128 devices in a mesh: row: 2 (over core), col: 2 (over x_hi), layer: 32 (over z, y, x_lo).
Axes of the slice: x: 4 (x_hi: 2, x_lo: 2; x = x_hi * 2 + x_lo), y: 4, z: 4, core: 2. Of those that a mesh axis runs over, the one named last changes fastest.
Arguments:
- a_tiles: bfloat16 [2, 2, 32, 64, 128, 128], P('row', 'col', 'layer'), may hold values from -6 to 6
- p_tiles: bfloat16 [2, 2, 32, 16, 128, 128], P('row', 'col', 'layer'), may hold values from -0.015625 to 0.015625
- pair_a: int32 [2, 2, 32, 2, 128, 16], P('row', 'col', 'layer'), may hold values from 0 to 63
- pair_p: int32 [2, 2, 32, 2, 128, 16], P('row', 'col', 'layer'), may hold values from 0 to 31
Outputs:
- c_tiles: bfloat16 [2, 2, 128, 128, 128], P('row', 'col', 'layer')
The draws below stay inside these ranges and needn't reach their ends.
All inputs are finite; a program needn't handle non-finite values.
Results may differ from the reference program's by a relative error of at most 0.0014.
Values may be sent and summed in bfloat16 or wider, within the bound.
A program may use at most 128 MiB of HBM per device.

```python
import jax
import jax.numpy as jnp
from jax import lax

TB = 128
SA = 64
SP = 16
FPC = 16
SC = 128
FAN = 32
N_ROW = 2
N_COL = 2
N_LAYER = 32


def set_ends(array, rng, smallest, high):
    longest = array.shape.index(max(array.shape))
    spots = []
    for shift in (0, 1):
        where = [jax.random.randint(jax.random.fold_in(rng, axis), (), 0, length) for axis, length in enumerate(array.shape)]
        where[longest] = (where[longest] + shift) % array.shape[longest]
        spots.append(tuple(where))
    return array.at[spots[0]].set(smallest).at[spots[1]].set(high)


def level_of(rng, dims, split, low, largest):
    def one(axis_at, parts):
        draws = jax.random.uniform(jax.random.fold_in(jax.random.fold_in(rng, 6), axis_at), (parts,), jnp.float32, low / len(split), largest / len(split))
        return jnp.repeat(jnp.exp(draws), dims[axis_at] // parts).reshape((-1,) + (1,) * (len(dims) - axis_at - 1))

    level = one(*split[0])
    for cut in split[1:]:
        level = level * one(*cut)
    return level


def gaussian(own_key, shape, scale, reach, pieces=(), kind=jnp.bfloat16):
    entries = scale * jax.random.normal(own_key, shape, jnp.float32)
    if pieces:
        entries = entries * level_of(own_key, shape, pieces, -0.22, 0.18)
    return jnp.clip(entries, -reach, reach).astype(kind)


def setup_inputs(seed: int = 0) -> dict:
    splits = jax.random.split(jax.random.key(seed), 5)
    a_tiles = gaussian(splits[0], (N_ROW, N_COL, N_LAYER, SA, TB, TB), 1.0, 6.0, ((0, 2), (1, 2), (2, 32)))
    p_tiles = gaussian(splits[1], (N_ROW, N_COL, N_LAYER, SP, TB, TB), (TB * FAN * N_LAYER) ** -0.5, 0.015625, ((0, 2), (1, 2), (2, 32)))
    pair_a = set_ends(jax.random.randint(splits[2], (N_ROW, N_COL, N_LAYER, N_COL, SC, FPC), 0, SA), jax.random.fold_in(splits[2], 1), 0, SA - 1).astype(jnp.int32)
    pair_p = set_ends(jax.random.randint(splits[3], (N_ROW, N_COL, N_LAYER, N_COL, SC, FPC), 0, N_ROW * SP), jax.random.fold_in(splits[3], 1), 0, (N_ROW * SP) - 1).astype(jnp.int32)
    return dict(a_tiles=a_tiles, p_tiles=p_tiles, pair_a=pair_a, pair_p=pair_p)


def reference(a_tiles, p_tiles, pair_a, pair_p):
    offsets = (jnp.arange(N_COL, dtype=jnp.int32) * SA)[:, None, None]

    def block(flat):
        r_index = flat // N_COL
        c_index = flat % N_COL
        a_row = lax.dynamic_index_in_dim(a_tiles, r_index, 0, keepdims=False)
        p_col = lax.dynamic_index_in_dim(p_tiles, c_index, 1, keepdims=False)
        pairs_a = lax.dynamic_index_in_dim(lax.dynamic_index_in_dim(pair_a, r_index, 0, keepdims=False), c_index, 0, keepdims=False)
        pairs_p = lax.dynamic_index_in_dim(lax.dynamic_index_in_dim(pair_p, r_index, 0, keepdims=False), c_index, 0, keepdims=False)
        a_layers = jnp.moveaxis(a_row, 1, 0)
        p_layers = jnp.moveaxis(p_col, 1, 0)

        def layer_step(total, inputs):
            a_layer, p_layer, index_a, index_p = inputs
            a_flat = a_layer.reshape(N_COL * SA, TB, TB)
            p_flat = p_layer.reshape(N_ROW * SP, TB, TB)
            glob_a = jnp.transpose(index_a + offsets, (1, 0, 2)).reshape(SC, FAN)
            glob_p = jnp.transpose(index_p, (1, 0, 2)).reshape(SC, FAN)

            def pair_step(acc, column):
                left = a_flat[column[0]].astype(jnp.float32)
                right = p_flat[column[1]].astype(jnp.float32)
                return acc + jnp.einsum("sij,sjk->sik", left, right), None

            total, _ = lax.scan(pair_step, total, (glob_a.T, glob_p.T))
            return total, None

        start = jnp.zeros((SC, TB, TB), jnp.float32)
        total, _ = lax.scan(layer_step, start, (a_layers, p_layers, pairs_a, pairs_p))
        return total.astype(jnp.bfloat16)

    blocks = lax.map(block, jnp.arange(N_ROW * N_COL, dtype=jnp.int32))
    return blocks.reshape(N_ROW, N_COL, SC, TB, TB)
```

```python
import jax
import jax.numpy as jnp
from jax import lax
from jax.experimental import pallas as pl
from jax.experimental.pallas import tpu as pltpu
from jax.sharding import PartitionSpec as P

TB = 128
FPC = 16
STEPS = 128.0
TOP = 32000.0
TINY = 2.0**-110
HALF = 4 * TB + 16
FULL = 8 * TB + 16
MAGIC = 12582912.0


def encode(tiles, message):
    spots = lax.broadcasted_iota(jnp.int32, (16, TB), 0)
    exponents = jnp.zeros((16, TB), jnp.float32)
    for i, tile in enumerate(tiles):
        top = jnp.maximum(jnp.max(jnp.abs(tile), axis=0, keepdims=True), TINY)
        exponent = jnp.floor(jnp.log2(top) * STEPS) + 2.0
        scaled = tile * (jnp.exp2(exponent * (-1.0 / STEPS)) * TOP)
        whole = ((scaled + MAGIC) - MAGIC).astype(jnp.int32)
        message[i * TB : (i + 1) * TB, :] = whole.astype(jnp.int16)
        exponents = jnp.where(spots == i, exponent, exponents)
    count = len(tiles)
    message[count * TB : count * TB + 16, :] = exponents.astype(jnp.int32).astype(jnp.int16)


def scales(message, count):
    exponents = message[count * TB : count * TB + 16, :].astype(jnp.int32).astype(jnp.float32)
    return jnp.exp2(exponents * (1.0 / STEPS)) * (1.0 / TOP)


def decode(message, scale, i):
    return message[i * TB : (i + 1) * TB, :].astype(jnp.int32).astype(jnp.float32) * scale[i : i + 1, :]


def decode_at(message, scale, i, count):
    spots = lax.broadcasted_iota(jnp.int32, (16, TB), 0)
    row = jnp.sum(jnp.where(spots == i, scale, 0.0), axis=0, keepdims=True)
    rows = pl.ds(pl.multiple_of(i * TB, TB), TB)
    return message[rows, :].astype(jnp.int32).astype(jnp.float32) * row


def kernel(
    pairs, a, p_own, out,
    p_all, p_land, pair_land, pair_mem, own_sum,
    far_out, far_in, near_out, near_in, mid_out, mid_in, last_out, last_in,
    local_sem, p_send, p_recv, pair_send, pair_recv,
    far_send, far_recv, near_send, near_recv, mid_send, mid_recv, last_send, last_recv,
):
    r = lax.axis_index("row")
    q = lax.axis_index("col")
    layer = lax.axis_index("layer")
    z = layer // 8
    y = (layer // 2) % 4
    x_lo = layer % 2

    def device(core, col, grid_zy, low):
        return (core, col, grid_zy * 2 + low)

    zy = z * 4 + y
    sibling = device(1 - r, q, zy, x_lo)
    partner = device(r, 1 - q, zy, x_lo)

    def across(phase, k):
        col = q * (1 - phase) + (1 - q) * phase
        low = x_lo * (1 - k) + (1 - x_lo) * k
        return device(r, col, zy, low)

    def places(o):
        first = z * (1 - o) + y * o
        second = y * (1 - o) + z * o
        return first, second

    def grid_zy(o, first, second):
        return first * (4 - 3 * o) + second * (1 + 3 * o)

    barrier = pltpu.get_barrier_semaphore()
    others = [sibling, partner, across(0, 1), across(1, 1)]
    for shift in (1, 2, 3):
        others.append(device(r, q, ((z + shift) % 4) * 4 + y, x_lo))
        others.append(device(r, q, z * 4 + (y + shift) % 4, x_lo))
    for other in others:
        pl.semaphore_signal(barrier, inc=1, device_id=other, device_id_type=pl.DeviceIdType.MESH)

    mine = pl.ds(r * 16, 16)
    theirs = pl.ds((1 - r) * 16, 16)
    own_copy = pltpu.make_async_copy(p_own, p_all.at[mine], local_sem.at[0])
    pair_copy = pltpu.make_async_copy(pairs.at[q], pair_mem.at[pl.ds(0, 16)], local_sem.at[1])
    own_copy.start()
    pair_copy.start()
    pl.semaphore_wait(barrier, len(others))

    def remote(src, dst, send, recv, to):
        return pltpu.make_async_remote_copy(
            src_ref=src, dst_ref=dst, send_sem=send, recv_sem=recv,
            device_id=to, device_id_type=pl.DeviceIdType.MESH,
        )

    to_sibling = remote(p_own, p_all.at[mine], p_send.at[0], p_recv.at[0], sibling)
    to_sibling.start()
    pairs_over = remote(pairs.at[1 - q], pair_land, pair_send, pair_recv, partner)
    pairs_over.start()
    to_partner = remote(p_own, p_land.at[mine], p_send.at[1], p_recv.at[1], partner)
    to_partner.start()
    forward = remote(p_land.at[mine], p_land.at[mine], p_send.at[2], p_recv.at[2], sibling)
    forward_in = remote(p_land.at[theirs], p_land.at[theirs], p_send.at[2], p_recv.at[2], sibling)
    own_copy.wait()
    pair_copy.wait()
    to_sibling.wait_recv()

    def far(slot, o, d, phase=None):
        first, second = places(o)
        to = device(r, q, grid_zy(o, (first + 1 + 2 * d) % 4, second), x_lo)
        return remote(far_out.at[slot], far_in.at[slot], far_send.at[slot], far_recv.at[slot], to)

    def near(slot, o, d):
        first, second = places(o)
        to = device(r, q, grid_zy(o, (first + 1 + 2 * d) % 4, second), x_lo)
        return remote(near_out.at[slot], near_in.at[slot], near_send.at[slot], near_recv.at[slot], to)

    def flip(second, k):
        high, low = second // 2, second % 2
        k_high, k_low = k // 2, k % 2
        high = high * (1 - k_high) + (1 - high) * k_high
        low = low * (1 - k_low) + (1 - low) * k_low
        return high * 2 + low

    def mid(phase, o, k):
        first, second = places(o)
        slot = (phase * 2 + o) * 3 + k - 1
        to = device(r, q, grid_zy(o, first, flip(second, k)), x_lo)
        return remote(mid_out.at[slot], mid_in.at[slot], mid_send.at[slot], mid_recv.at[slot], to)

    def last(phase, k):
        slot = phase * 2 + k - 1
        return remote(last_out.at[slot], last_in.at[slot], last_send.at[slot], last_recv.at[slot], across(phase, k))

    def product(phase, row, lane):
        total = None
        for g in range(FPC // 2):
            one = pair_mem[phase * 16 + row, lane + 2 * g]
            two = pair_mem[phase * 16 + row, lane + 2 * g + 1]
            left = jnp.concatenate([a[one >> 5], a[two >> 5]], axis=1)
            right = jnp.concatenate([p_all[phase * 32 + (one & 31)], p_all[phase * 32 + (two & 31)]], axis=0)
            part = jnp.dot(left, right, preferred_element_type=jnp.float32)
            total = part if total is None else total + part
        return total

    def far_step(phase):
        @pl.loop(0, 4)
        def _(i):
            o = i % 2
            first, second = places(o)
            h = second // 2
            g = (1 - h) * (1 - i // 2) + h * (i // 2)
            slot = ((phase * 2 + o) * 2 + g) * 2
            sums = [[], []]
            for n in range(2):
                row = grid_zy(o, (first + 2) % 4, g * 2 + n)
                for low in range(2):
                    for j in range(2):
                        sums[j].append(product(phase, row, o * 32 + low * 64 + j * 16))
            for d in range(2):
                encode(sums[d], far_out.at[slot + d])
                far(slot + d, o, d).start()

    def near_step(phase):
        @pl.loop(0, 8)
        def _(i):
            o = i % 2
            d = (i // 2) % 2
            first, second = places(o)
            h = second // 2
            g = (1 - h) * (1 - i // 4) + h * (i // 4)
            slot = ((phase * 2 + o) * 2 + g) * 2 + d
            far(slot, o, d).wait_recv()
            got = far_in.at[slot]
            scale = scales(got, 4)
            sums = []
            for n in range(2):
                row = grid_zy(o, (first + 1 + 2 * d) % 4, g * 2 + n)
                for low in range(2):
                    for j in range(2):
                        place = d * (1 - 2 * j) + j
                        tile = product(phase, row, o * 32 + low * 64 + place * 16)
                        if j == 0:
                            tile = tile + decode(got, scale, n * 2 + low)
                        sums.append(tile)
            encode(sums, near_out.at[slot])
            near(slot, o, d).start()

    def arrived(phase, o, second, low, j):
        slot = ((phase * 2 + o) * 2 + second // 2) * 2
        place = (second % 2) * 4 + low * 2
        plus, minus = near_in.at[slot], near_in.at[slot + 1]
        return decode_at(plus, scales(plus, 8), place + j, 8) + decode_at(minus, scales(minus, 8), place + 1 - j, 8)

    def wait_near(phase, o, g):
        for d in range(2):
            near(((phase * 2 + o) * 2 + g) * 2 + d, o, d).wait_recv()

    def mid_step(phase):
        @pl.loop(0, 3)
        def _(i):
            k = 2 + i - 3 * (i // 2)

            @pl.when(i == 0)
            def _():
                for o in range(2):
                    wait_near(phase, o, 1 - places(o)[1] // 2)

            @pl.when(i == 2)
            def _():
                for o in range(2):
                    wait_near(phase, o, places(o)[1] // 2)

            for o in range(2):
                first, second = places(o)
                there = flip(second, k)
                row = grid_zy(o, first, there)
                sums = []
                for low in range(2):
                    for j in range(2):
                        tile = product(phase, row, o * 32 + low * 64 + j * 16)
                        sums.append(tile + arrived(phase, o, there, low, j))
                encode(sums, mid_out.at[(phase * 2 + o) * 3 + k - 1])
                mid(phase, o, k).start()

    def last_step(phase):
        for o in range(2):
            for k in range(1, 4):
                mid(phase, o, k).wait_recv()
        for k in range(2):
            low = x_lo * (1 - k) + (1 - x_lo) * k
            sums = []
            for o in range(2):
                first, second = places(o)
                messages = [mid_in.at[(phase * 2 + o) * 3 + m] for m in range(3)]
                for j in range(2):
                    tile = product(phase, zy, o * 32 + low * 64 + j * 16)
                    tile = tile + arrived(phase, o, second, low, j)
                    for message in messages:
                        tile = tile + decode_at(message, scales(message, 4), low * 2 + j, 4)
                    sums.append(tile)
            if k == 1:
                encode(sums, last_out.at[phase * 2])
                last(phase, 1).start()
            else:
                @pl.when(phase == 0)
                def _():
                    for i, tile in enumerate(sums):
                        own_sum[i] = tile

                @pl.when(phase == 1)
                def _():
                    encode(sums, last_out.at[1])
                    last(1, 0).start()

    @pl.loop(0, 3)
    def _(step):
        @pl.when(step == 1)
        def _():
            to_partner.wait_recv()
            forward.start()
            pairs_over.wait_recv()
            move = pltpu.make_async_copy(pair_land, pair_mem.at[pl.ds(16, 16)], local_sem.at[1])
            move.start()
            move.wait()
            forward_in.wait_recv()

            @pl.loop(0, 32)
            def _(i):
                p_all[32 + i] = p_land[i]

        @pl.when(step < 2)
        def _():
            far_step(step)

        @pl.when(step > 0)
        def _():
            mid_step(step - 1)

        @pl.when(step < 2)
        def _():
            near_step(step)

        @pl.when(step > 0)
        def _():
            last_step(step - 1)

    for phase, k in ((0, 1), (1, 0), (1, 1)):
        last(phase, k).wait_recv()
    for i in range(4):
        total = own_sum[i]
        for slot in range(3):
            message = last_in.at[slot]
            total = total + decode(message, scales(message, 4), i)
        out[i] = total.astype(out.dtype)

    to_sibling.wait_send()
    to_partner.wait_send()
    forward.wait_send()
    pairs_over.wait_send()

    @pl.loop(0, 16)
    def _(i):
        o, d = (i // 4) % 2, i % 2
        far(i, o, d).wait_send()
        near(i, o, d).wait_send()

    for phase in range(2):
        for o in range(2):
            for k in range(1, 4):
                mid(phase, o, k).wait_send()
    for phase, k in ((0, 1), (1, 0), (1, 1)):
        last(phase, k).wait_send()


def on_device(a_tiles, p_tiles, pair_a, pair_p):
    pairs = (pair_a[0, 0, 0] * 32 + pair_p[0, 0, 0]).reshape(2, 16, TB)
    i16 = jnp.int16
    dma = pltpu.SemaphoreType.DMA
    vmem = pl.BlockSpec(memory_space=pltpu.VMEM)
    anywhere = pl.BlockSpec(memory_space=pl.ANY)
    out = pl.pallas_call(
        kernel,
        out_shape=jax.ShapeDtypeStruct((4, TB, TB), jnp.bfloat16),
        in_specs=[anywhere, vmem, anywhere],
        out_specs=vmem,
        scratch_shapes=[
            pltpu.VMEM((64, TB, TB), jnp.bfloat16),
            pltpu.VMEM((32, TB, TB), jnp.bfloat16),
            pltpu.VMEM((16, TB), jnp.int32),
            pltpu.SMEM((32, TB), jnp.int32),
            pltpu.VMEM((4, TB, TB), jnp.float32),
            pltpu.VMEM((16, HALF, TB), i16),
            pltpu.VMEM((16, HALF, TB), i16),
            pltpu.VMEM((16, FULL, TB), i16),
            pltpu.VMEM((16, FULL, TB), i16),
            pltpu.VMEM((12, HALF, TB), i16),
            pltpu.VMEM((12, HALF, TB), i16),
            pltpu.VMEM((3, HALF, TB), i16),
            pltpu.VMEM((3, HALF, TB), i16),
            dma((2,)), dma((3,)), dma((3,)), dma, dma,
            dma((16,)), dma((16,)), dma((16,)), dma((16,)),
            dma((12,)), dma((12,)), dma((3,)), dma((3,)),
        ],
        compiler_params=pltpu.CompilerParams(
            collective_id=0, has_side_effects=True, vmem_limit_bytes=56 << 20
        ),
        cost_estimate=pl.CostEstimate(flops=2 * 4096 * TB**3, bytes_accessed=4 << 20, transcendentals=0),
    )(pairs, a_tiles[0, 0, 0], p_tiles[0, 0, 0])
    return out[None, None]


def solution(mesh):
    tiles = P("row", "col", "layer", None, None, None)
    return jax.shard_map(
        on_device, mesh=mesh, in_specs=(tiles,) * 4,
        out_specs=P("row", "col", "layer", None, None), check_vma=False,
    )
```

```python
import jax
import jax.numpy as jnp
from jax import lax
from jax.experimental import pallas as pl
from jax.experimental.pallas import tpu as pltpu
from jax.sharding import PartitionSpec as P

TB = 128
FPC = 16
STEPS = 128.0
TOP = 32000.0
TINY = 2.0**-110
HALF = 4 * TB + 16
FULL = 8 * TB + 16
PAIR = 2 * TB + 16
MAGIC = 12582912.0

FAR, NEAR, SIDE, MID, HOME, TAKE, SPREAD, OWN = range(8)
ITEMS = (
    (FAR, 1, 0, 0),
    (FAR, 1, 1, 0),
    (FAR, 0, 0, 0),
    (FAR, 0, 1, 0),
    (NEAR, 1, 0, 1),
    (NEAR, 1, 1, 1),
    (NEAR, 1, 1, 0),
    (NEAR, 1, 0, 0),
    (NEAR, 0, 0, 1),
    (TAKE, 0, 0, 0),
    (NEAR, 0, 1, 1),
    (SPREAD, 0, 0, 0),
    (FAR, 2, 0, 0),
    (FAR, 2, 1, 0),
    (FAR, 3, 1, 0),
    (FAR, 3, 0, 0),
    (SIDE, 1, 0, 0),
    (NEAR, 2, 0, 0),
    (NEAR, 2, 1, 0),
    (NEAR, 2, 0, 1),
    (NEAR, 2, 1, 1),
    (SIDE, 1, 1, 0),
    (NEAR, 3, 0, 1),
    (NEAR, 3, 1, 0),
    (NEAR, 3, 0, 0),
    (NEAR, 3, 1, 1),
    (SIDE, 2, 0, 0),
    (NEAR, 0, 0, 0),
    (NEAR, 0, 1, 0),
    (SIDE, 2, 1, 0),
    (MID, 3, 0, 0),
    (MID, 3, 1, 0),
    (HOME, 0, 0, 0),
    (OWN, 0, 0, 0),
    (HOME, 0, 1, 0),
)

def encode(tiles, message):
    spots = lax.broadcasted_iota(jnp.int32, (16, TB), 0)
    exponents = jnp.zeros((16, TB), jnp.float32)
    for i, tile in enumerate(tiles):
        top = jnp.maximum(jnp.max(jnp.abs(tile), axis=0, keepdims=True), TINY)
        exponent = jnp.floor(jnp.log2(top) * STEPS) + 2.0
        scaled = tile * (jnp.exp2(exponent * (-1.0 / STEPS)) * TOP)
        whole = ((scaled + MAGIC) - MAGIC).astype(jnp.int32)
        message[i * TB : (i + 1) * TB, :] = whole.astype(jnp.int16)
        exponents = jnp.where(spots == i, exponent, exponents)
    count = len(tiles)
    message[count * TB : count * TB + 16, :] = exponents.astype(jnp.int32).astype(jnp.int16)


def scales(message, count):
    exponents = message[count * TB : count * TB + 16, :].astype(jnp.int32).astype(jnp.float32)
    return jnp.exp2(exponents * (1.0 / STEPS)) * (1.0 / TOP)


def decode(message, scale, i):
    return message[i * TB : (i + 1) * TB, :].astype(jnp.int32).astype(jnp.float32) * scale[i : i + 1, :]


def decode_at(message, scale, i, count):
    spots = lax.broadcasted_iota(jnp.int32, (16, TB), 0)
    row = jnp.sum(jnp.where(spots == i, scale, 0.0), axis=0, keepdims=True)
    rows = pl.ds(pl.multiple_of(i * TB, TB), TB)
    return message[rows, :].astype(jnp.int32).astype(jnp.float32) * row


def kernel(
    pairs, a, p_own, out,
    p_all, p_land, pair_land, pair_mem, own_sum,
    far_out, far_in, near_out, near_in, side_out, side_in, mid_out, mid_in, last_out, last_in,
    local_sem, p_send, p_recv, pair_send, pair_recv,
    far_send, far_recv, near_send, near_recv, side_send, side_recv, mid_send, mid_recv, last_send, last_recv,
):
    r = lax.axis_index("row")
    q = lax.axis_index("col")
    layer = lax.axis_index("layer")
    z = layer // 8
    y = (layer // 2) % 4
    x_lo = layer % 2
    zy = z * 4 + y

    def turned(bit, by):
        return bit * (1 - by) + (1 - bit) * by

    def flip(place, k):
        return turned(place // 2, k // 2) * 2 + turned(place % 2, k % 2)

    def device(core, col, at, low):
        return (core, col, at * 2 + low)

    def across(k):
        return device(r, turned(q, k // 2), zy, turned(x_lo, k % 2))

    def places(o):
        return z * (1 - o) + y * o, y * (1 - o) + z * o

    def grid_zy(o, first, second):
        return first * (4 - 3 * o) + second * (1 + 3 * o)

    sibling = device(1 - r, q, zy, x_lo)
    partner = across(2)

    barrier = pltpu.get_barrier_semaphore()
    others = [sibling, across(1), partner, across(3)]
    for shift in (1, 2, 3):
        others.append(device(r, q, ((z + shift) % 4) * 4 + y, x_lo))
        others.append(device(r, q, z * 4 + (y + shift) % 4, x_lo))
    for other in others:
        pl.semaphore_signal(barrier, inc=1, device_id=other, device_id_type=pl.DeviceIdType.MESH)

    mine = pl.ds(r * 16, 16)
    theirs = pl.ds((1 - r) * 16, 16)
    own_copy = pltpu.make_async_copy(p_own, p_all.at[mine], local_sem.at[0])
    pair_copy = pltpu.make_async_copy(pairs.at[q], pair_mem.at[pl.ds(0, 16)], local_sem.at[1])
    pair_move = pltpu.make_async_copy(pair_land, pair_mem.at[pl.ds(16, 16)], local_sem.at[2])
    own_copy.start()
    pair_copy.start()
    pl.semaphore_wait(barrier, len(others))

    def remote(src, dst, send, recv, to):
        return pltpu.make_async_remote_copy(
            src_ref=src, dst_ref=dst, send_sem=send, recv_sem=recv,
            device_id=to, device_id_type=pl.DeviceIdType.MESH,
        )

    to_sibling = remote(p_own, p_all.at[mine], p_send.at[0], p_recv.at[0], sibling)
    pairs_over = remote(pairs.at[1 - q], pair_land, pair_send, pair_recv, partner)
    to_partner = remote(p_own, p_land.at[mine], p_send.at[1], p_recv.at[1], partner)
    forward = remote(p_land.at[mine], p_land.at[mine], p_send.at[2], p_recv.at[2], sibling)
    forward_in = remote(p_land.at[theirs], p_land.at[theirs], p_send.at[2], p_recv.at[2], sibling)
    to_sibling.start()
    pairs_over.start()
    to_partner.start()
    own_copy.wait()
    pair_copy.wait()
    to_sibling.wait_recv()

    def along(o, d):
        first, second = places(o)
        return device(r, q, grid_zy(o, (first + 1 + 2 * d) % 4, second), x_lo)

    def far(k, o, d):
        at = (k * 2 + o) * 2 + d
        return remote(far_out.at[at], far_in.at[at], far_send.at[at], far_recv.at[at], along(o, d))

    def near(k, o, d):
        at = (k * 2 + o) * 2 + d
        return remote(near_out.at[at], near_in.at[at], near_send.at[at], near_recv.at[at], along(o, d))

    def side(k, g):
        at = (k - 1) * 2 + g
        return remote(side_out.at[at], side_in.at[at], side_send.at[at], side_recv.at[at], across(k))

    def mid(h, o, kk):
        at = (h * 2 + o) * 3 + kk - 1
        first, second = places(o)
        to = device(r, q, grid_zy(o, first, flip(second, kk)), x_lo)
        return remote(mid_out.at[at], mid_in.at[at], mid_send.at[at], mid_recv.at[at], to)

    last = remote(last_out, last_in, last_send, last_recv, across(3))

    def product(k, at, o, j):
        row = (k // 2) * 16 + at
        lane = turned(x_lo, k % 2) * 64 + o * 32 + j * 16
        first_p = (k // 2) * 32
        total = None
        for g in range(FPC // 2):
            one = pair_mem[row, lane + 2 * g]
            two = pair_mem[row, lane + 2 * g + 1]
            left = jnp.concatenate([a[one >> 5], a[two >> 5]], axis=1)
            right = jnp.concatenate([p_all[first_p + (one & 31)], p_all[first_p + (two & 31)]], axis=0)
            part = jnp.dot(left, right, preferred_element_type=jnp.float32)
            total = part if total is None else total + part
        return total

    def far_item(k, o):
        first, second = places(o)
        sums = [[], []]
        for n in range(4):
            at = grid_zy(o, (first + 2) % 4, n)
            for j in range(2):
                sums[j].append(product(k, at, o, j))
        for d in range(2):
            encode(sums[d], far_out.at[(k * 2 + o) * 2 + d])
            far(k, o, d).start()

    def near_item(k, o, d):
        first, second = places(o)
        far(k, o, d).wait_recv()
        got = far_in.at[(k * 2 + o) * 2 + d]
        scale = scales(got, 4)
        sums = []
        for n in range(4):
            at = grid_zy(o, (first + 1 + 2 * d) % 4, n)
            for j in range(2):
                tile = product(k, at, o, turned(j, d))
                if j == 0:
                    tile = tile + decode(got, scale, n)
                sums.append(tile)
        encode(sums, near_out.at[(k * 2 + o) * 2 + d])
        near(k, o, d).start()

    def mid_sums(k, g, extra):
        @pl.when(g == 0)
        def _():
            for o in range(2):
                for d in range(2):
                    near(k, o, d).wait_recv()

        for m in extra:
            side(m, g).wait_recv()
        sides = [side_in.at[(m - 1) * 2 + g] for m in extra]
        side_scales = [scales(message, 8) for message in sides]
        sums = []
        for o in range(2):
            first, second = places(o)
            plus, minus = near_in.at[(k * 2 + o) * 2], near_in.at[(k * 2 + o) * 2 + 1]
            plus_scale, minus_scale = scales(plus, 8), scales(minus, 8)
            for n in range(2):
                there = flip(second, (2 + n) * (1 - g) + (1 - n) * g)
                at = grid_zy(o, first, there)
                for j in range(2):
                    tile = product(k, at, o, j)
                    tile = tile + decode_at(plus, plus_scale, there * 2 + j, 8)
                    tile = tile + decode_at(minus, minus_scale, there * 2 + 1 - j, 8)
                    for message, scale in zip(sides, side_scales):
                        tile = tile + decode(message, scale, len(sums))
                    sums.append(tile)
        return sums

    def side_item(k, g):
        encode(mid_sums(k, g, ()), side_out.at[(k - 1) * 2 + g])
        side(k, g).start()

    def mid_item(k, h, g, extra):
        sums = mid_sums(k, g, extra)
        for o in range(2):
            kk = 2 - g
            encode(sums[o * 4 : o * 4 + 2], mid_out.at[(h * 2 + o) * 3 + kk - 1])
            mid(h, o, kk).start()

        @pl.when(g == 0)
        def _():
            for o in range(2):
                encode(sums[o * 4 + 2 : o * 4 + 4], mid_out.at[(h * 2 + o) * 3 + 2])
                mid(h, o, 3).start()

        @pl.when(g == 1)
        def _():
            for o in range(2):
                for j in range(2):
                    own_sum[h * 4 + o * 2 + j] = sums[o * 4 + 2 + j]

    def own_item(h):
        sums = []
        for o in range(2):
            messages = []
            for kk in range(1, 4):
                mid(h, o, kk).wait_recv()
                message = mid_in.at[(h * 2 + o) * 3 + kk - 1]
                messages.append((message, scales(message, 2)))
            for j in range(2):
                tile = own_sum[h * 4 + o * 2 + j]
                for message, scale in messages:
                    tile = tile + decode(message, scale, j)
                sums.append(tile)
        if h == 0:
            encode(sums, last_out)
            last.start()
        else:
            for i, tile in enumerate(sums):
                own_sum[4 + i] = tile

    def take_p():
        to_partner.wait_recv()
        forward.start()
        pairs_over.wait_recv()
        pair_move.start()

    def spread_p():
        pair_move.wait()
        forward_in.wait_recv()

        @pl.loop(0, 32)
        def _(i):
            p_all[32 + i] = p_land[i]

    @pl.loop(0, len(ITEMS))
    def _(i):
        code = 0
        for n, item in enumerate(ITEMS):
            code = jnp.where(i == n, ((item[0] * 4 + item[1]) * 2 + item[2]) * 2 + item[3], code)
        kind, k, u, d = code // 16, (code // 4) % 4, (code // 2) % 2, code % 2
        pl.when(kind == FAR)(lambda: far_item(k, u))
        pl.when(kind == NEAR)(lambda: near_item(k, u, d))
        pl.when(kind == SIDE)(lambda: side_item(k, u))
        pl.when(kind == MID)(lambda: mid_item(3, 0, u, ()))
        pl.when(kind == HOME)(lambda: mid_item(0, 1, u, (1, 2)))
        pl.when(kind == TAKE)(take_p)
        pl.when(kind == SPREAD)(spread_p)
        pl.when(kind == OWN)(lambda: own_item(0))
    own_item(1)

    last.wait_recv()
    scale = scales(last_in, 4)
    for i in range(4):
        out[i] = (own_sum[4 + i] + decode(last_in, scale, i)).astype(out.dtype)

    for copy in (to_sibling, to_partner, forward, pairs_over, last):
        copy.wait_send()

    @pl.loop(0, 16)
    def _(i):
        far(i // 4, (i // 2) % 2, i % 2).wait_send()
        near(i // 4, (i // 2) % 2, i % 2).wait_send()

    for k in (1, 2):
        for g in range(2):
            side(k, g).wait_send()
    for h in range(2):
        for o in range(2):
            for kk in range(1, 4):
                mid(h, o, kk).wait_send()


def on_device(a_tiles, p_tiles, pair_a, pair_p):
    pairs = (pair_a[0, 0, 0] * 32 + pair_p[0, 0, 0]).reshape(2, 16, TB)
    i16 = jnp.int16
    dma = pltpu.SemaphoreType.DMA
    vmem = pl.BlockSpec(memory_space=pltpu.VMEM)
    anywhere = pl.BlockSpec(memory_space=pl.ANY)
    out = pl.pallas_call(
        kernel,
        out_shape=jax.ShapeDtypeStruct((4, TB, TB), jnp.bfloat16),
        in_specs=[anywhere, vmem, anywhere],
        out_specs=vmem,
        scratch_shapes=[
            pltpu.VMEM((64, TB, TB), jnp.bfloat16),
            pltpu.VMEM((32, TB, TB), jnp.bfloat16),
            pltpu.VMEM((16, TB), jnp.int32),
            pltpu.SMEM((32, TB), jnp.int32),
            pltpu.VMEM((8, TB, TB), jnp.float32),
            pltpu.VMEM((16, HALF, TB), i16),
            pltpu.VMEM((16, HALF, TB), i16),
            pltpu.VMEM((16, FULL, TB), i16),
            pltpu.VMEM((16, FULL, TB), i16),
            pltpu.VMEM((4, FULL, TB), i16),
            pltpu.VMEM((4, FULL, TB), i16),
            pltpu.VMEM((12, PAIR, TB), i16),
            pltpu.VMEM((12, PAIR, TB), i16),
            pltpu.VMEM((HALF, TB), i16),
            pltpu.VMEM((HALF, TB), i16),
            dma((3,)), dma((3,)), dma((3,)), dma, dma,
            dma((16,)), dma((16,)), dma((16,)), dma((16,)),
            dma((4,)), dma((4,)), dma((12,)), dma((12,)), dma, dma,
        ],
        compiler_params=pltpu.CompilerParams(
            collective_id=0, has_side_effects=True, vmem_limit_bytes=56 << 20
        ),
        cost_estimate=pl.CostEstimate(flops=2 * 4096 * TB**3, bytes_accessed=4 << 20, transcendentals=0),
    )(pairs, a_tiles[0, 0, 0], p_tiles[0, 0, 0])
    return out[None, None]


def solution(mesh):
    tiles = P("row", "col", "layer", None, None, None)
    return jax.shard_map(
        on_device, mesh=mesh, in_specs=(tiles,) * 4,
        out_specs=P("row", "col", "layer", None, None), check_vma=False,
    )
```

```python
import jax
import jax.numpy as jnp
from jax import lax
from jax.experimental import pallas as pl
from jax.experimental.pallas import tpu as pltpu
from jax.sharding import PartitionSpec as P

TB = 128
FPC = 16
STEPS = 128.0
TOP = 32000.0
TINY = 2.0**-110
HALF = 4 * TB + 16
FULL = 8 * TB + 16
PAIR = 2 * TB + 16
MAGIC = 12582912.0

FAR, NEAR, SIDE, MID, HOME, TAKE, SPREAD, OWN = range(8)
ITEMS = (
    (FAR, 1, 0, 0),
    (FAR, 1, 1, 0),
    (FAR, 0, 0, 0),
    (FAR, 0, 1, 0),
    (NEAR, 1, 0, 1),
    (NEAR, 1, 1, 1),
    (NEAR, 1, 1, 0),
    (NEAR, 1, 0, 0),
    (NEAR, 0, 0, 1),
    (TAKE, 0, 0, 0),
    (NEAR, 0, 1, 1),
    (SPREAD, 0, 0, 0),
    (FAR, 2, 0, 0),
    (FAR, 2, 1, 0),
    (FAR, 3, 1, 0),
    (FAR, 3, 0, 0),
    (SIDE, 1, 0, 0),
    (NEAR, 2, 0, 0),
    (NEAR, 2, 1, 0),
    (NEAR, 2, 0, 1),
    (NEAR, 2, 1, 1),
    (SIDE, 1, 1, 0),
    (NEAR, 3, 0, 1),
    (NEAR, 3, 1, 0),
    (NEAR, 3, 0, 0),
    (NEAR, 3, 1, 1),
    (SIDE, 2, 0, 0),
    (NEAR, 0, 0, 0),
    (NEAR, 0, 1, 0),
    (SIDE, 2, 1, 0),
    (MID, 3, 0, 0),
    (MID, 3, 1, 0),
    (HOME, 0, 0, 0),
    (OWN, 0, 0, 0),
    (HOME, 0, 1, 0),
)

def encode(tiles, message):
    spots = lax.broadcasted_iota(jnp.int32, (16, TB), 0)
    exponents = jnp.zeros((16, TB), jnp.float32)
    for i, tile in enumerate(tiles):
        top = jnp.maximum(jnp.max(jnp.abs(tile), axis=0, keepdims=True), TINY)
        exponent = jnp.floor(jnp.log2(top) * STEPS) + 2.0
        scaled = tile * (jnp.exp2(exponent * (-1.0 / STEPS)) * TOP)
        whole = ((scaled + MAGIC) - MAGIC).astype(jnp.int32)
        message[i * TB : (i + 1) * TB, :] = whole.astype(jnp.int16)
        exponents = jnp.where(spots == i, exponent, exponents)
    count = len(tiles)
    message[count * TB : count * TB + 16, :] = exponents.astype(jnp.int32).astype(jnp.int16)


def scales(message, count):
    exponents = message[count * TB : count * TB + 16, :].astype(jnp.int32).astype(jnp.float32)
    return jnp.exp2(exponents * (1.0 / STEPS)) * (1.0 / TOP)


def decode(message, scale, i):
    return message[i * TB : (i + 1) * TB, :].astype(jnp.int32).astype(jnp.float32) * scale[i : i + 1, :]


def decode_at(message, scale, i, count):
    spots = lax.broadcasted_iota(jnp.int32, (16, TB), 0)
    row = jnp.sum(jnp.where(spots == i, scale, 0.0), axis=0, keepdims=True)
    rows = pl.ds(pl.multiple_of(i * TB, TB), TB)
    return message[rows, :].astype(jnp.int32).astype(jnp.float32) * row


def kernel(
    pair_a, pair_p, a_own, p_own, out,
    a, p_all, p_land, pair_land, mem_a, mem_p, own_sum,
    far_out, far_in, near_out, near_in, side_out, side_in, mid_out, mid_in, last_out, last_in,
    local_sem, p_send, p_recv, pair_send, pair_recv,
    far_send, far_recv, near_send, near_recv, side_send, side_recv, mid_send, mid_recv, last_send, last_recv,
):
    r = lax.axis_index("row")
    q = lax.axis_index("col")
    layer = lax.axis_index("layer")
    z = layer // 8
    y = (layer // 2) % 4
    x_lo = layer % 2
    zy = z * 4 + y

    def turned(bit, by):
        return bit * (1 - by) + (1 - bit) * by

    def flip(place, k):
        return turned(place // 2, k // 2) * 2 + turned(place % 2, k % 2)

    def device(core, col, at, low):
        return (core, col, at * 2 + low)

    def across(k):
        return device(r, turned(q, k // 2), zy, turned(x_lo, k % 2))

    def places(o):
        return z * (1 - o) + y * o, y * (1 - o) + z * o

    def grid_zy(o, first, second):
        return first * (4 - 3 * o) + second * (1 + 3 * o)

    sibling = device(1 - r, q, zy, x_lo)
    partner = across(2)

    barrier = pltpu.get_barrier_semaphore()
    others = [sibling, across(1), partner, across(3)]
    for shift in (1, 2, 3):
        others.append(device(r, q, ((z + shift) % 4) * 4 + y, x_lo))
        others.append(device(r, q, z * 4 + (y + shift) % 4, x_lo))
    for other in others:
        pl.semaphore_signal(barrier, inc=1, device_id=other, device_id_type=pl.DeviceIdType.MESH)

    mine = pl.ds(r * 16, 16)
    theirs = pl.ds((1 - r) * 16, 16)
    own_copy = pltpu.make_async_copy(p_own, p_all.at[mine], local_sem.at[0])
    pair_copies = [
        pltpu.make_async_copy(pair.at[q], mem.at[pl.ds(0, 16)], local_sem.at[1 + i])
        for i, (pair, mem) in enumerate(((pair_a, mem_a), (pair_p, mem_p)))
    ]
    pair_moves = [
        pltpu.make_async_copy(pair_land.at[i], mem.at[pl.ds(16, 16)], local_sem.at[3 + i])
        for i, mem in enumerate((mem_a, mem_p))
    ]
    a_copy = pltpu.make_async_copy(a_own, a, local_sem.at[5])
    own_copy.start()
    a_copy.start()
    for copy in pair_copies:
        copy.start()
    pl.semaphore_wait(barrier, len(others))

    def remote(src, dst, send, recv, to):
        return pltpu.make_async_remote_copy(
            src_ref=src, dst_ref=dst, send_sem=send, recv_sem=recv,
            device_id=to, device_id_type=pl.DeviceIdType.MESH,
        )

    to_sibling = remote(p_own, p_all.at[mine], p_send.at[0], p_recv.at[0], sibling)
    pairs_over = [
        remote(pair.at[1 - q], pair_land.at[i], pair_send.at[i], pair_recv.at[i], partner)
        for i, pair in enumerate((pair_a, pair_p))
    ]
    to_partner = remote(p_own, p_land.at[mine], p_send.at[1], p_recv.at[1], partner)
    forward = remote(p_land.at[mine], p_land.at[mine], p_send.at[2], p_recv.at[2], sibling)
    forward_in = remote(p_land.at[theirs], p_land.at[theirs], p_send.at[2], p_recv.at[2], sibling)
    to_sibling.start()
    for copy in pairs_over:
        copy.start()
    to_partner.start()
    own_copy.wait()
    a_copy.wait()
    for copy in pair_copies:
        copy.wait()
    to_sibling.wait_recv()

    def along(o, d):
        first, second = places(o)
        return device(r, q, grid_zy(o, (first + 1 + 2 * d) % 4, second), x_lo)

    def far(k, o, d):
        at = (k * 2 + o) * 2 + d
        return remote(far_out.at[at], far_in.at[at], far_send.at[at], far_recv.at[at], along(o, d))

    def near(k, o, d):
        at = (k * 2 + o) * 2 + d
        return remote(near_out.at[at], near_in.at[at], near_send.at[at], near_recv.at[at], along(o, d))

    def side(k, g):
        at = (k - 1) * 2 + g
        return remote(side_out.at[at], side_in.at[at], side_send.at[at], side_recv.at[at], across(k))

    def mid(h, o, kk):
        at = (h * 2 + o) * 3 + kk - 1
        first, second = places(o)
        to = device(r, q, grid_zy(o, first, flip(second, kk)), x_lo)
        return remote(mid_out.at[at], mid_in.at[at], mid_send.at[at], mid_recv.at[at], to)

    last = remote(last_out, last_in, last_send, last_recv, across(3))

    def product(k, at, o, j):
        row = (k // 2) * 16
        lane = at * 8 + turned(x_lo, k % 2) * 4 + o * 2 + j
        first_p = (k // 2) * 32
        total = None
        for g in range(FPC // 2):
            one, two = row + 2 * g, row + 2 * g + 1
            left = jnp.concatenate([a[mem_a[one, lane]], a[mem_a[two, lane]]], axis=1)
            right = jnp.concatenate([p_all[first_p + mem_p[one, lane]], p_all[first_p + mem_p[two, lane]]], axis=0)
            part = jnp.dot(left, right, preferred_element_type=jnp.float32)
            total = part if total is None else total + part
        return total

    def far_item(k, o):
        first, second = places(o)
        sums = [[], []]
        for n in range(4):
            at = grid_zy(o, (first + 2) % 4, n)
            for j in range(2):
                sums[j].append(product(k, at, o, j))
        for d in range(2):
            encode(sums[d], far_out.at[(k * 2 + o) * 2 + d])
            far(k, o, d).start()

    def near_item(k, o, d):
        first, second = places(o)
        far(k, o, d).wait_recv()
        got = far_in.at[(k * 2 + o) * 2 + d]
        scale = scales(got, 4)
        sums = []
        for n in range(4):
            at = grid_zy(o, (first + 1 + 2 * d) % 4, n)
            for j in range(2):
                tile = product(k, at, o, turned(j, d))
                if j == 0:
                    tile = tile + decode(got, scale, n)
                sums.append(tile)
        encode(sums, near_out.at[(k * 2 + o) * 2 + d])
        near(k, o, d).start()

    def mid_sums(k, g, extra):
        @pl.when(g == 0)
        def _():
            for o in range(2):
                for d in range(2):
                    near(k, o, d).wait_recv()

        for m in extra:
            side(m, g).wait_recv()
        sides = [side_in.at[(m - 1) * 2 + g] for m in extra]
        side_scales = [scales(message, 8) for message in sides]
        sums = []
        for o in range(2):
            first, second = places(o)
            plus, minus = near_in.at[(k * 2 + o) * 2], near_in.at[(k * 2 + o) * 2 + 1]
            plus_scale, minus_scale = scales(plus, 8), scales(minus, 8)
            for n in range(2):
                there = flip(second, (2 + n) * (1 - g) + (1 - n) * g)
                at = grid_zy(o, first, there)
                for j in range(2):
                    tile = product(k, at, o, j)
                    tile = tile + decode_at(plus, plus_scale, there * 2 + j, 8)
                    tile = tile + decode_at(minus, minus_scale, there * 2 + 1 - j, 8)
                    for message, scale in zip(sides, side_scales):
                        tile = tile + decode(message, scale, len(sums))
                    sums.append(tile)
        return sums

    def side_item(k, g):
        encode(mid_sums(k, g, ()), side_out.at[(k - 1) * 2 + g])
        side(k, g).start()

    def mid_item(k, h, g, extra):
        sums = mid_sums(k, g, extra)
        for o in range(2):
            kk = 2 - g
            encode(sums[o * 4 : o * 4 + 2], mid_out.at[(h * 2 + o) * 3 + kk - 1])
            mid(h, o, kk).start()

        @pl.when(g == 0)
        def _():
            for o in range(2):
                encode(sums[o * 4 + 2 : o * 4 + 4], mid_out.at[(h * 2 + o) * 3 + 2])
                mid(h, o, 3).start()

        @pl.when(g == 1)
        def _():
            for o in range(2):
                for j in range(2):
                    own_sum[h * 4 + o * 2 + j] = sums[o * 4 + 2 + j]

    def own_item(h):
        sums = []
        for o in range(2):
            messages = []
            for kk in range(1, 4):
                mid(h, o, kk).wait_recv()
                message = mid_in.at[(h * 2 + o) * 3 + kk - 1]
                messages.append((message, scales(message, 2)))
            for j in range(2):
                tile = own_sum[h * 4 + o * 2 + j]
                for message, scale in messages:
                    tile = tile + decode(message, scale, j)
                sums.append(tile)
        if h == 0:
            encode(sums, last_out)
            last.start()
        else:
            for i, tile in enumerate(sums):
                own_sum[4 + i] = tile

    def take_p():
        to_partner.wait_recv()
        forward.start()
        for copy in pairs_over:
            copy.wait_recv()
        for copy in pair_moves:
            copy.start()

    def spread_p():
        for copy in pair_moves:
            copy.wait()
        forward_in.wait_recv()

        @pl.loop(0, 32)
        def _(i):
            p_all[32 + i] = p_land[i]

    @pl.loop(0, len(ITEMS))
    def _(i):
        word = 0
        for n in range(0, len(ITEMS), 4):
            codes = [((item[0] * 4 + item[1]) * 2 + item[2]) * 2 + item[3] for item in ITEMS[n : n + 4]]
            word = jnp.where(i // 4 == n // 4, sum(code << (7 * at) for at, code in enumerate(codes)), word)
        code = (word >> (7 * (i % 4))) & 127
        kind, k, u, d = code // 16, (code // 4) % 4, (code // 2) % 2, code % 2
        pl.when(kind == FAR)(lambda: far_item(k, u))
        pl.when(kind == NEAR)(lambda: near_item(k, u, d))
        pl.when(kind == SIDE)(lambda: side_item(k, u))
        pl.when(kind == MID)(lambda: mid_item(3, 0, u, ()))
        pl.when(kind == HOME)(lambda: mid_item(0, 1, u, (1, 2)))
        pl.when(kind == TAKE)(take_p)
        pl.when(kind == SPREAD)(spread_p)
        pl.when(kind == OWN)(lambda: own_item(0))
    own_item(1)

    last.wait_recv()
    scale = scales(last_in, 4)
    for i in range(4):
        out[i] = (own_sum[4 + i] + decode(last_in, scale, i)).astype(out.dtype)

    for copy in (to_sibling, to_partner, forward, *pairs_over, last):
        copy.wait_send()

    @pl.loop(0, 16)
    def _(i):
        far(i // 4, (i // 2) % 2, i % 2).wait_send()
        near(i // 4, (i // 2) % 2, i % 2).wait_send()

    for k in (1, 2):
        for g in range(2):
            side(k, g).wait_send()
    for h in range(2):
        for o in range(2):
            for kk in range(1, 4):
                mid(h, o, kk).wait_send()


def on_device(a_tiles, p_tiles, pair_a, pair_p):
    lists = [jnp.transpose(pair[0, 0, 0], (0, 2, 1)) for pair in (pair_a, pair_p)]
    i16 = jnp.int16
    dma = pltpu.SemaphoreType.DMA
    vmem = pl.BlockSpec(memory_space=pltpu.VMEM)
    anywhere = pl.BlockSpec(memory_space=pl.ANY)
    out = pl.pallas_call(
        kernel,
        out_shape=jax.ShapeDtypeStruct((4, TB, TB), jnp.bfloat16),
        in_specs=[anywhere] * 4,
        out_specs=vmem,
        scratch_shapes=[
            pltpu.VMEM((64, TB, TB), jnp.bfloat16),
            pltpu.VMEM((64, TB, TB), jnp.bfloat16),
            pltpu.VMEM((32, TB, TB), jnp.bfloat16),
            pltpu.VMEM((2, 16, TB), jnp.int32),
            pltpu.SMEM((32, TB), jnp.int32),
            pltpu.SMEM((32, TB), jnp.int32),
            pltpu.VMEM((8, TB, TB), jnp.float32),
            pltpu.VMEM((16, HALF, TB), i16),
            pltpu.VMEM((16, HALF, TB), i16),
            pltpu.VMEM((16, FULL, TB), i16),
            pltpu.VMEM((16, FULL, TB), i16),
            pltpu.VMEM((4, FULL, TB), i16),
            pltpu.VMEM((4, FULL, TB), i16),
            pltpu.VMEM((12, PAIR, TB), i16),
            pltpu.VMEM((12, PAIR, TB), i16),
            pltpu.VMEM((HALF, TB), i16),
            pltpu.VMEM((HALF, TB), i16),
            dma((6,)), dma((3,)), dma((3,)), dma((2,)), dma((2,)),
            dma((16,)), dma((16,)), dma((16,)), dma((16,)),
            dma((4,)), dma((4,)), dma((12,)), dma((12,)), dma, dma,
        ],
        compiler_params=pltpu.CompilerParams(
            collective_id=0, has_side_effects=True, vmem_limit_bytes=56 << 20
        ),
        cost_estimate=pl.CostEstimate(flops=2 * 4096 * TB**3, bytes_accessed=4 << 20, transcendentals=0),
    )(*lists, a_tiles[0, 0, 0], p_tiles[0, 0, 0])
    return out[None, None]


def solution(mesh):
    tiles = P("row", "col", "layer", None, None, None)
    return jax.shard_map(
        on_device, mesh=mesh, in_specs=(tiles,) * 4,
        out_specs=P("row", "col", "layer", None, None), check_vma=False,
    )
```

```python
import jax
import jax.numpy as jnp
from jax import lax
from jax.experimental import pallas as pl
from jax.experimental.pallas import tpu as pltpu
from jax.sharding import PartitionSpec as P

TB = 128
FPC = 16
STEPS = 128.0
TOP = 32000.0
TINY = 2.0**-110
HALF = 4 * TB + 16
FULL = 8 * TB + 16
PAIR = 2 * TB + 16
MAGIC = 12582912.0

FAR, NEAR, SIDE, MID, HOME, TAKE, SPREAD, OWN = range(8)
ITEMS = (
    (FAR, 1, 0, 0),
    (FAR, 1, 1, 0),
    (FAR, 0, 0, 0),
    (FAR, 0, 1, 0),
    (NEAR, 1, 0, 1),
    (NEAR, 1, 1, 1),
    (NEAR, 1, 1, 0),
    (NEAR, 1, 0, 0),
    (NEAR, 0, 0, 1),
    (TAKE, 0, 0, 0),
    (NEAR, 0, 1, 1),
    (SPREAD, 0, 0, 0),
    (FAR, 2, 0, 0),
    (FAR, 2, 1, 0),
    (FAR, 3, 1, 0),
    (FAR, 3, 0, 0),
    (SIDE, 1, 0, 0),
    (NEAR, 2, 0, 0),
    (NEAR, 2, 1, 0),
    (NEAR, 2, 0, 1),
    (NEAR, 2, 1, 1),
    (SIDE, 1, 1, 0),
    (NEAR, 3, 0, 1),
    (NEAR, 3, 1, 0),
    (NEAR, 3, 0, 0),
    (NEAR, 3, 1, 1),
    (SIDE, 2, 0, 0),
    (NEAR, 0, 0, 0),
    (NEAR, 0, 1, 0),
    (SIDE, 2, 1, 0),
    (MID, 3, 0, 0),
    (MID, 3, 1, 0),
    (HOME, 0, 0, 0),
    (OWN, 0, 0, 0),
    (HOME, 0, 1, 0),
)

def encode(tiles, message):
    spots = lax.broadcasted_iota(jnp.int32, (16, TB), 0)
    exponents = jnp.zeros((16, TB), jnp.float32)
    for i, tile in enumerate(tiles):
        top = jnp.maximum(jnp.max(jnp.abs(tile), axis=0, keepdims=True), TINY)
        exponent = jnp.floor(jnp.log2(top) * STEPS) + 2.0
        scaled = tile * (jnp.exp2(exponent * (-1.0 / STEPS)) * TOP)
        whole = ((scaled + MAGIC) - MAGIC).astype(jnp.int32)
        message[i * TB : (i + 1) * TB, :] = whole.astype(jnp.int16)
        exponents = jnp.where(spots == i, exponent, exponents)
    count = len(tiles)
    message[count * TB : count * TB + 16, :] = exponents.astype(jnp.int32).astype(jnp.int16)


def scales(message, count):
    exponents = message[count * TB : count * TB + 16, :].astype(jnp.int32).astype(jnp.float32)
    return jnp.exp2(exponents * (1.0 / STEPS)) * (1.0 / TOP)


def decode(message, scale, i):
    return message[i * TB : (i + 1) * TB, :].astype(jnp.int32).astype(jnp.float32) * scale[i : i + 1, :]


def decode_at(message, scale, i, count):
    spots = lax.broadcasted_iota(jnp.int32, (16, TB), 0)
    row = jnp.sum(jnp.where(spots == i, scale, 0.0), axis=0, keepdims=True)
    rows = pl.ds(pl.multiple_of(i * TB, TB), TB)
    return message[rows, :].astype(jnp.int32).astype(jnp.float32) * row


def kernel(
    pair_a, pair_p, a_own, p_own, out,
    a, p_all, p_land, pair_land, mem_a, mem_p, own_sum,
    far_out, far_in, near_out, near_in, side_out, side_in, mid_out, mid_in, last_out, last_in,
    local_sem, p_send, p_recv, pair_send, pair_recv,
    far_send, far_recv, near_send, near_recv, side_send, side_recv, mid_send, mid_recv, last_send, last_recv,
):
    r = lax.axis_index("row")
    q = lax.axis_index("col")
    layer = lax.axis_index("layer")
    z = layer // 8
    y = (layer // 2) % 4
    x_lo = layer % 2
    zy = z * 4 + y

    def turned(bit, by):
        return bit * (1 - by) + (1 - bit) * by

    def flip(place, k):
        return turned(place // 2, k // 2) * 2 + turned(place % 2, k % 2)

    def device(core, col, at, low):
        return (core, col, at * 2 + low)

    def across(k):
        return device(r, turned(q, k // 2), zy, turned(x_lo, k % 2))

    def places(o):
        return z * (1 - o) + y * o, y * (1 - o) + z * o

    def grid_zy(o, first, second):
        return first * (4 - 3 * o) + second * (1 + 3 * o)

    sibling = device(1 - r, q, zy, x_lo)
    partner = across(2)

    barrier = pltpu.get_barrier_semaphore()
    others = [sibling, across(1), partner, across(3)]
    for shift in (1, 2, 3):
        others.append(device(r, q, ((z + shift) % 4) * 4 + y, x_lo))
        others.append(device(r, q, z * 4 + (y + shift) % 4, x_lo))
    for other in others:
        pl.semaphore_signal(barrier, inc=1, device_id=other, device_id_type=pl.DeviceIdType.MESH)

    mine = pl.ds(r * 16, 16)
    theirs = pl.ds((1 - r) * 16, 16)
    own_copy = pltpu.make_async_copy(p_own, p_all.at[mine], local_sem.at[0])
    pair_copies = [
        pltpu.make_async_copy(pair.at[q], mem.at[pl.ds(0, 16)], local_sem.at[1 + i])
        for i, (pair, mem) in enumerate(((pair_a, mem_a), (pair_p, mem_p)))
    ]
    pair_moves = [
        pltpu.make_async_copy(pair_land.at[i], mem.at[pl.ds(16, 16)], local_sem.at[3 + i])
        for i, mem in enumerate((mem_a, mem_p))
    ]
    a_copy = pltpu.make_async_copy(a_own, a, local_sem.at[5])
    own_copy.start()
    a_copy.start()
    for copy in pair_copies:
        copy.start()
    pl.semaphore_wait(barrier, len(others))

    def remote(src, dst, send, recv, to):
        return pltpu.make_async_remote_copy(
            src_ref=src, dst_ref=dst, send_sem=send, recv_sem=recv,
            device_id=to, device_id_type=pl.DeviceIdType.MESH,
        )

    to_sibling = remote(p_own, p_all.at[mine], p_send.at[0], p_recv.at[0], sibling)
    pairs_over = [
        remote(pair.at[1 - q], pair_land.at[i], pair_send.at[i], pair_recv.at[i], partner)
        for i, pair in enumerate((pair_a, pair_p))
    ]
    to_partner = remote(p_own, p_land.at[mine], p_send.at[1], p_recv.at[1], partner)
    forward = remote(p_land.at[mine], p_land.at[mine], p_send.at[2], p_recv.at[2], sibling)
    forward_in = remote(p_land.at[theirs], p_land.at[theirs], p_send.at[2], p_recv.at[2], sibling)
    to_sibling.start()
    for copy in pairs_over:
        copy.start()
    to_partner.start()
    own_copy.wait()
    a_copy.wait()
    for copy in pair_copies:
        copy.wait()
    to_sibling.wait_recv()

    def along(o, d):
        first, second = places(o)
        return device(r, q, grid_zy(o, (first + 1 + 2 * d) % 4, second), x_lo)

    def far(k, o, d):
        at = (k * 2 + o) * 2 + d
        return remote(far_out.at[at], far_in.at[at], far_send.at[at], far_recv.at[at], along(o, d))

    def near(k, o, d):
        at = (k * 2 + o) * 2 + d
        return remote(near_out.at[at], near_in.at[at], near_send.at[at], near_recv.at[at], along(o, d))

    def side(k, g):
        at = (k - 1) * 2 + g
        return remote(side_out.at[at], side_in.at[at], side_send.at[at], side_recv.at[at], across(k))

    def mid(h, o, kk):
        at = (h * 2 + o) * 3 + kk - 1
        first, second = places(o)
        to = device(r, q, grid_zy(o, first, flip(second, kk)), x_lo)
        return remote(mid_out.at[at], mid_in.at[at], mid_send.at[at], mid_recv.at[at], to)

    last = remote(last_out, last_in, last_send, last_recv, across(3))

    def product(k, at, o, j):
        row = (k // 2) * 16
        lane = at * 8 + turned(x_lo, k % 2) * 4 + o * 2 + j
        first_p = (k // 2) * 32
        total = None
        for g in range(FPC // 2):
            one, two = row + 2 * g, row + 2 * g + 1
            left = jnp.concatenate([a[mem_a[one, lane]], a[mem_a[two, lane]]], axis=1)
            right = jnp.concatenate([p_all[first_p + mem_p[one, lane]], p_all[first_p + mem_p[two, lane]]], axis=0)
            part = jnp.dot(left, right, preferred_element_type=jnp.float32)
            total = part if total is None else total + part
        return total

    def far_item(k, o):
        first, second = places(o)
        sums = [[], []]
        for n in range(4):
            at = grid_zy(o, (first + 2) % 4, n)
            for j in range(2):
                sums[j].append(product(k, at, o, j))
        for d in range(2):
            encode(sums[d], far_out.at[(k * 2 + o) * 2 + d])
            far(k, o, d).start()

    def near_item(k, o, d):
        first, second = places(o)
        far(k, o, d).wait_recv()
        got = far_in.at[(k * 2 + o) * 2 + d]
        scale = scales(got, 4)
        sums = []
        for n in range(4):
            at = grid_zy(o, (first + 1 + 2 * d) % 4, n)
            for j in range(2):
                tile = product(k, at, o, turned(j, d))
                if j == 0:
                    tile = tile + decode(got, scale, n)
                sums.append(tile)
        encode(sums, near_out.at[(k * 2 + o) * 2 + d])
        near(k, o, d).start()

    def mid_sums(k, g, extra):
        @pl.when(g == 0)
        def _():
            for o in range(2):
                for d in range(2):
                    near(k, o, d).wait_recv()

        for m in extra:
            side(m, g).wait_recv()
        sides = [side_in.at[(m - 1) * 2 + g] for m in extra]
        side_scales = [scales(message, 8) for message in sides]
        sums = []
        for o in range(2):
            first, second = places(o)
            plus, minus = near_in.at[(k * 2 + o) * 2], near_in.at[(k * 2 + o) * 2 + 1]
            plus_scale, minus_scale = scales(plus, 8), scales(minus, 8)
            for n in range(2):
                there = flip(second, (2 + n) * (1 - g) + (1 - n) * g)
                at = grid_zy(o, first, there)
                for j in range(2):
                    tile = product(k, at, o, j)
                    tile = tile + decode_at(plus, plus_scale, there * 2 + j, 8)
                    tile = tile + decode_at(minus, minus_scale, there * 2 + 1 - j, 8)
                    for message, scale in zip(sides, side_scales):
                        tile = tile + decode(message, scale, len(sums))
                    sums.append(tile)
        return sums

    def side_item(k, g):
        encode(mid_sums(k, g, ()), side_out.at[(k - 1) * 2 + g])
        side(k, g).start()

    def mid_item(k, h, g, extra):
        sums = mid_sums(k, g, extra)
        for o in range(2):
            kk = 2 - g
            encode(sums[o * 4 : o * 4 + 2], mid_out.at[(h * 2 + o) * 3 + kk - 1])
            mid(h, o, kk).start()

        @pl.when(g == 0)
        def _():
            for o in range(2):
                encode(sums[o * 4 + 2 : o * 4 + 4], mid_out.at[(h * 2 + o) * 3 + 2])
                mid(h, o, 3).start()

        @pl.when(g == 1)
        def _():
            for o in range(2):
                for j in range(2):
                    own_sum[h * 4 + o * 2 + j] = sums[o * 4 + 2 + j]

    def own_item(h):
        sums = []
        for o in range(2):
            messages = []
            for kk in range(1, 4):
                mid(h, o, kk).wait_recv()
                message = mid_in.at[(h * 2 + o) * 3 + kk - 1]
                messages.append((message, scales(message, 2)))
            for j in range(2):
                tile = own_sum[h * 4 + o * 2 + j]
                for message, scale in messages:
                    tile = tile + decode(message, scale, j)
                sums.append(tile)
        if h == 0:
            encode(sums, last_out)
            last.start()
        else:
            for i, tile in enumerate(sums):
                own_sum[4 + i] = tile

    def take_p():
        to_partner.wait_recv()
        forward.start()
        for copy in pairs_over:
            copy.wait_recv()
        for copy in pair_moves:
            copy.start()

    def spread_p():
        for copy in pair_moves:
            copy.wait()
        forward_in.wait_recv()

        @pl.loop(0, 32)
        def _(i):
            p_all[32 + i] = p_land[i]

    @pl.loop(0, len(ITEMS))
    def _(i):
        word = 0
        for n in range(0, len(ITEMS), 4):
            codes = [((item[0] * 4 + item[1]) * 2 + item[2]) * 2 + item[3] for item in ITEMS[n : n + 4]]
            word = jnp.where(i // 4 == n // 4, sum(code << (7 * at) for at, code in enumerate(codes)), word)
        code = (word >> (7 * (i % 4))) & 127
        kind, k, u, d = code // 16, (code // 4) % 4, (code // 2) % 2, code % 2
        pl.when(kind == FAR)(lambda: far_item(k, turned(u, r)))
        pl.when(kind == NEAR)(lambda: near_item(k, turned(u, r), turned(d, r)))

        @pl.when(kind >= SIDE)
        def _():
            pl.when(kind == SIDE)(lambda: side_item(k, u))
            pl.when(kind == MID)(lambda: mid_item(3, 0, u, ()))
            pl.when(kind == HOME)(lambda: mid_item(0, 1, u, (1, 2)))
            pl.when(kind == TAKE)(take_p)
            pl.when(kind == SPREAD)(spread_p)
            pl.when(kind == OWN)(lambda: own_item(0))
    own_item(1)

    last.wait_recv()
    scale = scales(last_in, 4)
    for i in range(4):
        out[i] = (own_sum[4 + i] + decode(last_in, scale, i)).astype(out.dtype)

    for copy in (to_sibling, to_partner, forward, *pairs_over, last):
        copy.wait_send()

    @pl.loop(0, 16)
    def _(i):
        far(i // 4, (i // 2) % 2, i % 2).wait_send()
        near(i // 4, (i // 2) % 2, i % 2).wait_send()

    for k in (1, 2):
        for g in range(2):
            side(k, g).wait_send()
    for h in range(2):
        for o in range(2):
            for kk in range(1, 4):
                mid(h, o, kk).wait_send()


def on_device(a_tiles, p_tiles, pair_a, pair_p):
    lists = [jnp.transpose(pair[0, 0, 0], (0, 2, 1)) for pair in (pair_a, pair_p)]
    i16 = jnp.int16
    dma = pltpu.SemaphoreType.DMA
    vmem = pl.BlockSpec(memory_space=pltpu.VMEM)
    anywhere = pl.BlockSpec(memory_space=pl.ANY)
    out = pl.pallas_call(
        kernel,
        out_shape=jax.ShapeDtypeStruct((4, TB, TB), jnp.bfloat16),
        in_specs=[anywhere] * 4,
        out_specs=vmem,
        scratch_shapes=[
            pltpu.VMEM((64, TB, TB), jnp.bfloat16),
            pltpu.VMEM((64, TB, TB), jnp.bfloat16),
            pltpu.VMEM((32, TB, TB), jnp.bfloat16),
            pltpu.VMEM((2, 16, TB), jnp.int32),
            pltpu.SMEM((32, TB), jnp.int32),
            pltpu.SMEM((32, TB), jnp.int32),
            pltpu.VMEM((8, TB, TB), jnp.float32),
            pltpu.VMEM((16, HALF, TB), i16),
            pltpu.VMEM((16, HALF, TB), i16),
            pltpu.VMEM((16, FULL, TB), i16),
            pltpu.VMEM((16, FULL, TB), i16),
            pltpu.VMEM((4, FULL, TB), i16),
            pltpu.VMEM((4, FULL, TB), i16),
            pltpu.VMEM((12, PAIR, TB), i16),
            pltpu.VMEM((12, PAIR, TB), i16),
            pltpu.VMEM((HALF, TB), i16),
            pltpu.VMEM((HALF, TB), i16),
            dma((6,)), dma((3,)), dma((3,)), dma((2,)), dma((2,)),
            dma((16,)), dma((16,)), dma((16,)), dma((16,)),
            dma((4,)), dma((4,)), dma((12,)), dma((12,)), dma, dma,
        ],
        compiler_params=pltpu.CompilerParams(
            collective_id=0, has_side_effects=True, vmem_limit_bytes=56 << 20
        ),
        cost_estimate=pl.CostEstimate(flops=2 * 4096 * TB**3, bytes_accessed=4 << 20, transcendentals=0),
    )(*lists, a_tiles[0, 0, 0], p_tiles[0, 0, 0])
    return out[None, None]


def solution(mesh):
    tiles = P("row", "col", "layer", None, None, None)
    return jax.shard_map(
        on_device, mesh=mesh, in_specs=(tiles,) * 4,
        out_specs=P("row", "col", "layer", None, None), check_vma=False,
    )
```

```python
import jax
import jax.numpy as jnp
from jax import lax
from jax.experimental import pallas as pl
from jax.experimental.pallas import tpu as pltpu
from jax.sharding import PartitionSpec as P

TB = 128
FPC = 16
STEPS = 128.0
TOP = 32000.0
TINY = 2.0**-110
HALF = 4 * TB + 16
FULL = 8 * TB + 16
PAIR = 2 * TB + 16
MAGIC = 12582912.0

FAR, NEAR, SIDE, MID, HOME, TAKE, SPREAD, OWN = range(8)
ITEMS = (
    (FAR, 1, 0, 0),
    (FAR, 1, 1, 0),
    (FAR, 0, 0, 0),
    (FAR, 0, 1, 0),
    (NEAR, 1, 0, 1),
    (NEAR, 1, 1, 1),
    (NEAR, 1, 1, 0),
    (NEAR, 1, 0, 0),
    (NEAR, 0, 0, 1),
    (TAKE, 0, 0, 0),
    (NEAR, 0, 1, 1),
    (SPREAD, 0, 0, 0),
    (FAR, 2, 0, 0),
    (FAR, 2, 1, 0),
    (FAR, 3, 1, 0),
    (FAR, 3, 0, 0),
    (SIDE, 1, 0, 0),
    (NEAR, 2, 0, 0),
    (NEAR, 2, 1, 0),
    (NEAR, 2, 0, 1),
    (NEAR, 2, 1, 1),
    (SIDE, 1, 1, 0),
    (NEAR, 3, 0, 1),
    (NEAR, 3, 1, 0),
    (NEAR, 3, 0, 0),
    (NEAR, 3, 1, 1),
    (SIDE, 2, 0, 0),
    (NEAR, 0, 0, 0),
    (NEAR, 0, 1, 0),
    (SIDE, 2, 1, 0),
    (MID, 3, 0, 0),
    (MID, 3, 1, 0),
    (HOME, 0, 0, 0),
    (OWN, 0, 0, 0),
    (HOME, 0, 1, 0),
)

def encode(tiles, message):
    spots = lax.broadcasted_iota(jnp.int32, (16, TB), 0)
    exponents = jnp.zeros((16, TB), jnp.float32)
    for i, tile in enumerate(tiles):
        top = jnp.maximum(jnp.max(jnp.abs(tile), axis=0, keepdims=True), TINY)
        exponent = jnp.floor(jnp.log2(top) * STEPS) + 2.0
        scaled = tile * (jnp.exp2(exponent * (-1.0 / STEPS)) * TOP)
        whole = ((scaled + MAGIC) - MAGIC).astype(jnp.int32)
        message[i * TB : (i + 1) * TB, :] = whole.astype(jnp.int16)
        exponents = jnp.where(spots == i, exponent, exponents)
    count = len(tiles)
    message[count * TB : count * TB + 16, :] = exponents.astype(jnp.int32).astype(jnp.int16)


def scales(message, count):
    exponents = message[count * TB : count * TB + 16, :].astype(jnp.int32).astype(jnp.float32)
    return jnp.exp2(exponents * (1.0 / STEPS)) * (1.0 / TOP)


def decode(message, scale, i):
    return message[i * TB : (i + 1) * TB, :].astype(jnp.int32).astype(jnp.float32) * scale[i : i + 1, :]


def decode_at(message, scale, i, count):
    spots = lax.broadcasted_iota(jnp.int32, (16, TB), 0)
    row = jnp.sum(jnp.where(spots == i, scale, 0.0), axis=0, keepdims=True)
    rows = pl.ds(pl.multiple_of(i * TB, TB), TB)
    return message[rows, :].astype(jnp.int32).astype(jnp.float32) * row


def kernel(
    pair_a, pair_p, a_own, p_own, out,
    a, p_all, p_land, pair_land, mem_a, mem_p, own_sum,
    far_out, far_in, near_out, near_in, side_out, side_in, mid_out, mid_in, last_out, last_in,
    local_sem, p_send, p_recv, pair_send, pair_recv,
    far_send, far_recv, near_send, near_recv, side_send, side_recv, mid_send, mid_recv, last_send, last_recv,
):
    r = lax.axis_index("row")
    q = lax.axis_index("col")
    layer = lax.axis_index("layer")
    z = layer // 8
    y = (layer // 2) % 4
    x_lo = layer % 2
    zy = z * 4 + y

    def turned(bit, by):
        return bit * (1 - by) + (1 - bit) * by

    def flip(place, k):
        return turned(place // 2, k // 2) * 2 + turned(place % 2, k % 2)

    def device(core, col, at, low):
        return (core, col, at * 2 + low)

    def across(k):
        return device(r, turned(q, k // 2), zy, turned(x_lo, k % 2))

    def places(o):
        return z * (1 - o) + y * o, y * (1 - o) + z * o

    def grid_zy(o, first, second):
        return first * (4 - 3 * o) + second * (1 + 3 * o)

    sibling = device(1 - r, q, zy, x_lo)
    partner = across(2)

    barrier = pltpu.get_barrier_semaphore()
    others = [sibling, across(1), partner, across(3)]
    for shift in (1, 2, 3):
        others.append(device(r, q, ((z + shift) % 4) * 4 + y, x_lo))
        others.append(device(r, q, z * 4 + (y + shift) % 4, x_lo))
    for other in others:
        pl.semaphore_signal(barrier, inc=1, device_id=other, device_id_type=pl.DeviceIdType.MESH)

    mine = pl.ds(r * 16, 16)
    theirs = pl.ds((1 - r) * 16, 16)
    own_copy = pltpu.make_async_copy(p_own, p_all.at[mine], local_sem.at[0])
    pair_copies = [
        pltpu.make_async_copy(pair.at[q], mem.at[pl.ds(0, 16)], local_sem.at[1 + i])
        for i, (pair, mem) in enumerate(((pair_a, mem_a), (pair_p, mem_p)))
    ]
    pair_moves = [
        pltpu.make_async_copy(pair_land.at[i], mem.at[pl.ds(16, 16)], local_sem.at[3 + i])
        for i, mem in enumerate((mem_a, mem_p))
    ]
    a_copy = pltpu.make_async_copy(a_own, a, local_sem.at[5])
    own_copy.start()
    a_copy.start()
    for copy in pair_copies:
        copy.start()
    pl.semaphore_wait(barrier, len(others))

    def remote(src, dst, send, recv, to):
        return pltpu.make_async_remote_copy(
            src_ref=src, dst_ref=dst, send_sem=send, recv_sem=recv,
            device_id=to, device_id_type=pl.DeviceIdType.MESH,
        )

    to_sibling = remote(p_own, p_all.at[mine], p_send.at[0], p_recv.at[0], sibling)
    pairs_over = [
        remote(pair.at[1 - q], pair_land.at[i], pair_send.at[i], pair_recv.at[i], partner)
        for i, pair in enumerate((pair_a, pair_p))
    ]
    to_partner = remote(p_own, p_land.at[mine], p_send.at[1], p_recv.at[1], partner)
    forward = remote(p_land.at[mine], p_land.at[mine], p_send.at[2], p_recv.at[2], sibling)
    forward_in = remote(p_land.at[theirs], p_land.at[theirs], p_send.at[2], p_recv.at[2], sibling)
    to_sibling.start()
    for copy in pairs_over:
        copy.start()
    to_partner.start()
    own_copy.wait()
    a_copy.wait()
    for copy in pair_copies:
        copy.wait()
    to_sibling.wait_recv()

    def along(o, d):
        first, second = places(o)
        return device(r, q, grid_zy(o, (first + 1 + 2 * d) % 4, second), x_lo)

    def far(k, o, d):
        at = (k * 2 + o) * 2 + d
        return remote(far_out.at[at], far_in.at[at], far_send.at[at], far_recv.at[at], along(o, d))

    def near(k, o, d):
        at = (k * 2 + o) * 2 + d
        return remote(near_out.at[at], near_in.at[at], near_send.at[at], near_recv.at[at], along(o, d))

    def side(k, g):
        at = (k - 1) * 2 + g
        return remote(side_out.at[at], side_in.at[at], side_send.at[at], side_recv.at[at], across(k))

    def mid(h, o, kk):
        at = (h * 2 + o) * 3 + kk - 1
        first, second = places(o)
        to = device(r, q, grid_zy(o, first, flip(second, kk)), x_lo)
        return remote(mid_out.at[at], mid_in.at[at], mid_send.at[at], mid_recv.at[at], to)

    last = remote(last_out, last_in, last_send, last_recv, across(3))

    def product(k, at, o, j):
        row = (k // 2) * 16
        lane = at * 8 + turned(x_lo, k % 2) * 4 + o * 2 + j
        first_p = (k // 2) * 32
        total = None
        for g in range(FPC // 2):
            one, two = row + 2 * g, row + 2 * g + 1
            left = jnp.concatenate([a[mem_a[one, lane]], a[mem_a[two, lane]]], axis=1)
            right = jnp.concatenate([p_all[first_p + mem_p[one, lane]], p_all[first_p + mem_p[two, lane]]], axis=0)
            part = jnp.dot(left, right, preferred_element_type=jnp.float32)
            total = part if total is None else total + part
        return total

    def far_item(k, o):
        first, second = places(o)
        sums = [[], []]
        for n in range(4):
            at = grid_zy(o, (first + 2) % 4, n)
            for j in range(2):
                sums[j].append(product(k, at, o, j))
        for d in range(2):
            encode(sums[d], far_out.at[(k * 2 + o) * 2 + d])
        for d in range(2):
            far(k, o, d).start()

    def near_item(k, o, d):
        first, second = places(o)
        far(k, o, d).wait_recv()
        got = far_in.at[(k * 2 + o) * 2 + d]
        scale = scales(got, 4)
        sums = []
        for n in range(4):
            at = grid_zy(o, (first + 1 + 2 * d) % 4, n)
            for j in range(2):
                tile = product(k, at, o, turned(j, d))
                if j == 0:
                    tile = tile + decode(got, scale, n)
                sums.append(tile)
        encode(sums, near_out.at[(k * 2 + o) * 2 + d])
        near(k, o, d).start()

    def mid_sums(k, g, extra):
        @pl.when(g == 0)
        def _():
            for o in range(2):
                for d in range(2):
                    near(k, o, d).wait_recv()

        for m in extra:
            side(m, g).wait_recv()
        sides = [side_in.at[(m - 1) * 2 + g] for m in extra]
        side_scales = [scales(message, 8) for message in sides]
        sums = []
        for o in range(2):
            first, second = places(o)
            plus, minus = near_in.at[(k * 2 + o) * 2], near_in.at[(k * 2 + o) * 2 + 1]
            plus_scale, minus_scale = scales(plus, 8), scales(minus, 8)
            for n in range(2):
                there = flip(second, (2 + n) * (1 - g) + (1 - n) * g)
                at = grid_zy(o, first, there)
                for j in range(2):
                    tile = product(k, at, o, j)
                    tile = tile + decode_at(plus, plus_scale, there * 2 + j, 8)
                    tile = tile + decode_at(minus, minus_scale, there * 2 + 1 - j, 8)
                    for message, scale in zip(sides, side_scales):
                        tile = tile + decode(message, scale, len(sums))
                    sums.append(tile)
        return sums

    def side_item(k, g):
        encode(mid_sums(k, g, ()), side_out.at[(k - 1) * 2 + g])
        side(k, g).start()

    def mid_item(k, h, g, extra):
        sums = mid_sums(k, g, extra)
        kk = 2 - g
        for o in range(2):
            encode(sums[o * 4 : o * 4 + 2], mid_out.at[(h * 2 + o) * 3 + kk - 1])
            encode(sums[o * 4 + 2 : o * 4 + 4], mid_out.at[((h * 2 + o) * 3 + 2) * (1 - g) + 12 * g])
            for j in range(2):
                own_sum[h * 4 + o * 2 + j] = sums[o * 4 + 2 + j]
        for o in range(2):
            mid(h, o, kk).start()

        @pl.when(g == 0)
        def _():
            for o in range(2):
                mid(h, o, 3).start()

    def own_item(h):
        sums = []
        for o in range(2):
            messages = []
            for kk in range(1, 4):
                mid(h, o, kk).wait_recv()
                message = mid_in.at[(h * 2 + o) * 3 + kk - 1]
                messages.append((message, scales(message, 2)))
            for j in range(2):
                tile = own_sum[h * 4 + o * 2 + j]
                for message, scale in messages:
                    tile = tile + decode(message, scale, j)
                sums.append(tile)
        if h == 0:
            encode(sums, last_out)
            last.start()
        else:
            for i, tile in enumerate(sums):
                own_sum[4 + i] = tile

    def take_p():
        to_partner.wait_recv()
        forward.start()
        for copy in pairs_over:
            copy.wait_recv()
        for copy in pair_moves:
            copy.start()

    def spread_p():
        for copy in pair_moves:
            copy.wait()
        forward_in.wait_recv()

        @pl.loop(0, 32)
        def _(i):
            p_all[32 + i] = p_land[i]

    @pl.loop(0, len(ITEMS))
    def _(i):
        word = 0
        for n in range(0, len(ITEMS), 4):
            codes = [((item[0] * 4 + item[1]) * 2 + item[2]) * 2 + item[3] for item in ITEMS[n : n + 4]]
            word = jnp.where(i // 4 == n // 4, sum(code << (7 * at) for at, code in enumerate(codes)), word)
        code = (word >> (7 * (i % 4))) & 127
        kind, k, u, d = code // 16, (code // 4) % 4, (code // 2) % 2, code % 2
        pl.when(kind == FAR)(lambda: far_item(k, turned(u, r)))
        pl.when(kind == NEAR)(lambda: near_item(k, turned(u, r), turned(d, r)))

        @pl.when(kind >= SIDE)
        def _():
            pl.when(kind == SIDE)(lambda: side_item(k, u))
            pl.when(kind == MID)(lambda: mid_item(3, 0, u, ()))
            pl.when(kind == HOME)(lambda: mid_item(0, 1, u, (1, 2)))
            pl.when(kind == TAKE)(take_p)
            pl.when(kind == SPREAD)(spread_p)
            pl.when(kind == OWN)(lambda: own_item(0))
    own_item(1)

    last.wait_recv()
    scale = scales(last_in, 4)
    for i in range(4):
        out[i] = (own_sum[4 + i] + decode(last_in, scale, i)).astype(out.dtype)

    for copy in (to_sibling, to_partner, forward, *pairs_over, last):
        copy.wait_send()

    @pl.loop(0, 16)
    def _(i):
        far(i // 4, (i // 2) % 2, i % 2).wait_send()
        near(i // 4, (i // 2) % 2, i % 2).wait_send()

    for k in (1, 2):
        for g in range(2):
            side(k, g).wait_send()
    for h in range(2):
        for o in range(2):
            for kk in range(1, 4):
                mid(h, o, kk).wait_send()


def on_device(a_tiles, p_tiles, pair_a, pair_p):
    lists = [jnp.transpose(pair[0, 0, 0], (0, 2, 1)) for pair in (pair_a, pair_p)]
    i16 = jnp.int16
    dma = pltpu.SemaphoreType.DMA
    vmem = pl.BlockSpec(memory_space=pltpu.VMEM)
    anywhere = pl.BlockSpec(memory_space=pl.ANY)
    out = pl.pallas_call(
        kernel,
        out_shape=jax.ShapeDtypeStruct((4, TB, TB), jnp.bfloat16),
        in_specs=[anywhere] * 4,
        out_specs=vmem,
        scratch_shapes=[
            pltpu.VMEM((64, TB, TB), jnp.bfloat16),
            pltpu.VMEM((64, TB, TB), jnp.bfloat16),
            pltpu.VMEM((32, TB, TB), jnp.bfloat16),
            pltpu.VMEM((2, 16, TB), jnp.int32),
            pltpu.SMEM((32, TB), jnp.int32),
            pltpu.SMEM((32, TB), jnp.int32),
            pltpu.VMEM((8, TB, TB), jnp.float32),
            pltpu.VMEM((16, HALF, TB), i16),
            pltpu.VMEM((16, HALF, TB), i16),
            pltpu.VMEM((16, FULL, TB), i16),
            pltpu.VMEM((16, FULL, TB), i16),
            pltpu.VMEM((4, FULL, TB), i16),
            pltpu.VMEM((4, FULL, TB), i16),
            pltpu.VMEM((13, PAIR, TB), i16),
            pltpu.VMEM((12, PAIR, TB), i16),
            pltpu.VMEM((HALF, TB), i16),
            pltpu.VMEM((HALF, TB), i16),
            dma((6,)), dma((3,)), dma((3,)), dma((2,)), dma((2,)),
            dma((16,)), dma((16,)), dma((16,)), dma((16,)),
            dma((4,)), dma((4,)), dma((12,)), dma((12,)), dma, dma,
        ],
        compiler_params=pltpu.CompilerParams(
            collective_id=0, has_side_effects=True, vmem_limit_bytes=56 << 20
        ),
        cost_estimate=pl.CostEstimate(flops=2 * 4096 * TB**3, bytes_accessed=4 << 20, transcendentals=0),
    )(*lists, a_tiles[0, 0, 0], p_tiles[0, 0, 0])
    return out[None, None]


def solution(mesh):
    tiles = P("row", "col", "layer", None, None, None)
    return jax.shard_map(
        on_device, mesh=mesh, in_specs=(tiles,) * 4,
        out_specs=P("row", "col", "layer", None, None), check_vma=False,
    )
```

```python
import jax
import jax.numpy as jnp
from jax import lax
from jax.experimental import pallas as pl
from jax.experimental.pallas import tpu as pltpu
from jax.sharding import PartitionSpec as P

TB = 128
FPC = 16
STEPS = 128.0
TOP = 32000.0
TINY = 2.0**-110
HALF = 4 * TB + 16
FULL = 8 * TB + 16
PAIR = 2 * TB + 16
MAGIC = 12582912.0

FAR, NEAR, SIDE, MID, HOME, TAKE, SPREAD, OWN = range(8)
ITEMS = (
    (FAR, 1, 0, 0),
    (FAR, 1, 1, 0),
    (FAR, 0, 0, 0),
    (FAR, 0, 1, 0),
    (NEAR, 1, 0, 1),
    (NEAR, 1, 1, 1),
    (NEAR, 1, 1, 0),
    (NEAR, 1, 0, 0),
    (NEAR, 0, 0, 1),
    (TAKE, 0, 0, 0),
    (NEAR, 0, 1, 1),
    (SPREAD, 0, 0, 0),
    (FAR, 2, 0, 0),
    (FAR, 2, 1, 0),
    (FAR, 3, 1, 0),
    (FAR, 3, 0, 0),
    (SIDE, 1, 0, 0),
    (NEAR, 2, 0, 0),
    (NEAR, 2, 1, 0),
    (NEAR, 2, 0, 1),
    (NEAR, 2, 1, 1),
    (SIDE, 1, 1, 0),
    (NEAR, 3, 0, 1),
    (NEAR, 3, 1, 0),
    (NEAR, 3, 0, 0),
    (NEAR, 3, 1, 1),
    (SIDE, 2, 0, 0),
    (NEAR, 0, 0, 0),
    (NEAR, 0, 1, 0),
    (SIDE, 2, 1, 0),
    (MID, 3, 0, 0),
    (MID, 3, 1, 0),
    (HOME, 0, 0, 0),
    (OWN, 0, 0, 0),
    (HOME, 0, 1, 0),
)

def encode(tiles, message):
    spots = lax.broadcasted_iota(jnp.int32, (16, TB), 0)
    exponents = jnp.zeros((16, TB), jnp.float32)
    for i, tile in enumerate(tiles):
        top = jnp.maximum(jnp.max(jnp.abs(tile), axis=0, keepdims=True), TINY)
        exponent = jnp.floor(jnp.log2(top) * STEPS) + 2.0
        scaled = tile * (jnp.exp2(exponent * (-1.0 / STEPS)) * TOP)
        whole = ((scaled + MAGIC) - MAGIC).astype(jnp.int32)
        message[i * TB : (i + 1) * TB, :] = whole.astype(jnp.int16)
        exponents = jnp.where(spots == i, exponent, exponents)
    count = len(tiles)
    message[count * TB : count * TB + 16, :] = exponents.astype(jnp.int32).astype(jnp.int16)


def scales(message, count):
    exponents = message[count * TB : count * TB + 16, :].astype(jnp.int32).astype(jnp.float32)
    return jnp.exp2(exponents * (1.0 / STEPS)) * (1.0 / TOP)


def decode(message, scale, i):
    return message[i * TB : (i + 1) * TB, :].astype(jnp.int32).astype(jnp.float32) * scale[i : i + 1, :]


def decode_at(message, scale, i, count):
    spots = lax.broadcasted_iota(jnp.int32, (16, TB), 0)
    row = jnp.sum(jnp.where(spots == i, scale, 0.0), axis=0, keepdims=True)
    rows = pl.ds(pl.multiple_of(i * TB, TB), TB)
    return message[rows, :].astype(jnp.int32).astype(jnp.float32) * row


def kernel(
    pair_a, pair_p, a_own, p_own, out,
    a, p_all, p_land, pair_land, mem_a, mem_p, own_sum,
    far_out, far_in, near_out, near_in, side_out, side_in, mid_out, mid_in, last_out, last_in,
    local_sem, p_send, p_recv, pair_send, pair_recv,
    far_send, far_recv, near_send, near_recv, side_send, side_recv, mid_send, mid_recv, last_send, last_recv,
):
    r = lax.axis_index("row")
    q = lax.axis_index("col")
    layer = lax.axis_index("layer")
    z = layer // 8
    y = (layer // 2) % 4
    x_lo = layer % 2
    zy = z * 4 + y

    def turned(bit, by):
        return bit * (1 - by) + (1 - bit) * by

    def flip(place, k):
        return turned(place // 2, k // 2) * 2 + turned(place % 2, k % 2)

    def device(core, col, at, low):
        return (core, col, at * 2 + low)

    def across(k):
        return device(r, turned(q, k // 2), zy, turned(x_lo, k % 2))

    def places(o):
        return z * (1 - o) + y * o, y * (1 - o) + z * o

    def grid_zy(o, first, second):
        return first * (4 - 3 * o) + second * (1 + 3 * o)

    sibling = device(1 - r, q, zy, x_lo)
    partner = across(2)

    barrier = pltpu.get_barrier_semaphore()
    others = [sibling, across(1), partner, across(3)]
    for shift in (1, 2, 3):
        others.append(device(r, q, ((z + shift) % 4) * 4 + y, x_lo))
        others.append(device(r, q, z * 4 + (y + shift) % 4, x_lo))
    for other in others:
        pl.semaphore_signal(barrier, inc=1, device_id=other, device_id_type=pl.DeviceIdType.MESH)

    mine = pl.ds(r * 16, 16)
    theirs = pl.ds((1 - r) * 16, 16)
    own_copy = pltpu.make_async_copy(p_own, p_all.at[mine], local_sem.at[0])
    pair_copies = [
        pltpu.make_async_copy(pair.at[q], mem.at[pl.ds(0, 16)], local_sem.at[1 + i])
        for i, (pair, mem) in enumerate(((pair_a, mem_a), (pair_p, mem_p)))
    ]
    pair_moves = [
        pltpu.make_async_copy(pair_land.at[i], mem.at[pl.ds(16, 16)], local_sem.at[3 + i])
        for i, mem in enumerate((mem_a, mem_p))
    ]
    a_copy = pltpu.make_async_copy(a_own, a, local_sem.at[5])
    own_copy.start()
    a_copy.start()
    for copy in pair_copies:
        copy.start()
    pl.semaphore_wait(barrier, len(others))

    def remote(src, dst, send, recv, to):
        return pltpu.make_async_remote_copy(
            src_ref=src, dst_ref=dst, send_sem=send, recv_sem=recv,
            device_id=to, device_id_type=pl.DeviceIdType.MESH,
        )

    to_sibling = remote(p_own, p_all.at[mine], p_send.at[0], p_recv.at[0], sibling)
    pairs_over = [
        remote(pair.at[1 - q], pair_land.at[i], pair_send.at[i], pair_recv.at[i], partner)
        for i, pair in enumerate((pair_a, pair_p))
    ]
    to_partner = remote(p_own, p_land.at[mine], p_send.at[1], p_recv.at[1], partner)
    forward = remote(p_land.at[mine], p_land.at[mine], p_send.at[2], p_recv.at[2], sibling)
    forward_in = remote(p_land.at[theirs], p_land.at[theirs], p_send.at[2], p_recv.at[2], sibling)
    to_sibling.start()
    for copy in pairs_over:
        copy.start()
    to_partner.start()
    own_copy.wait()
    a_copy.wait()
    for copy in pair_copies:
        copy.wait()
    to_sibling.wait_recv()

    def along(o, d):
        first, second = places(o)
        return device(r, q, grid_zy(o, (first + 1 + 2 * d) % 4, second), x_lo)

    def far(k, o, d):
        at = (k * 2 + o) * 2 + d
        return remote(far_out.at[at], far_in.at[at], far_send.at[at], far_recv.at[at], along(o, d))

    def near(k, o, d):
        at = (k * 2 + o) * 2 + d
        return remote(near_out.at[at], near_in.at[at], near_send.at[at], near_recv.at[at], along(o, d))

    def side(k, g):
        at = (k - 1) * 2 + g
        return remote(side_out.at[at], side_in.at[at], side_send.at[at], side_recv.at[at], across(k))

    def mid(h, o, kk):
        at = (h * 2 + o) * 3 + kk - 1
        first, second = places(o)
        to = device(r, q, grid_zy(o, first, flip(second, kk)), x_lo)
        return remote(mid_out.at[at], mid_in.at[at], mid_send.at[at], mid_recv.at[at], to)

    last = remote(last_out, last_in, last_send, last_recv, across(3))

    def product(k, at, o, j):
        row = (k // 2) * 16
        lane = at * 8 + turned(x_lo, k % 2) * 4 + o * 2 + j
        first_p = (k // 2) * 32
        total = None
        for g in range(FPC // 2):
            one, two = row + 2 * g, row + 2 * g + 1
            left = jnp.concatenate([a[mem_a[one, lane]], a[mem_a[two, lane]]], axis=1)
            right = jnp.concatenate([p_all[first_p + mem_p[one, lane]], p_all[first_p + mem_p[two, lane]]], axis=0)
            part = jnp.dot(left, right, preferred_element_type=jnp.float32)
            total = part if total is None else total + part
        return total

    def far_item(k, o):
        first, second = places(o)
        sums = [[], []]
        for n in range(4):
            at = grid_zy(o, (first + 2) % 4, n)
            for j in range(2):
                sums[j].append(product(k, at, o, j))
        for d in range(2):
            encode(sums[d], far_out.at[(k * 2 + o) * 2 + d])
        for d in range(2):
            far(k, o, d).start()

    def near_item(k, o, d):
        first, second = places(o)
        far(k, o, d).wait_recv()
        got = far_in.at[(k * 2 + o) * 2 + d]
        scale = scales(got, 4)
        sums = []
        for n in range(4):
            at = grid_zy(o, (first + 1 + 2 * d) % 4, n)
            for j in range(2):
                tile = product(k, at, o, turned(j, d))
                if j == 0:
                    tile = tile + decode(got, scale, n)
                sums.append(tile)
        encode(sums, near_out.at[(k * 2 + o) * 2 + d])
        near(k, o, d).start()

    def mid_sums(k, g, extra):
        @pl.when(g == 0)
        def _():
            for o in range(2):
                for d in range(2):
                    near(k, o, d).wait_recv()

        for m in extra:
            side(m, g).wait_recv()
        sides = [side_in.at[(m - 1) * 2 + g] for m in extra]
        side_scales = [scales(message, 8) for message in sides]
        sums = []
        for o in range(2):
            first, second = places(o)
            plus, minus = near_in.at[(k * 2 + o) * 2], near_in.at[(k * 2 + o) * 2 + 1]
            plus_scale, minus_scale = scales(plus, 8), scales(minus, 8)
            for n in range(2):
                there = flip(second, (2 + n) * (1 - g) + (1 - n) * g)
                at = grid_zy(o, first, there)
                for j in range(2):
                    tile = product(k, at, o, j)
                    tile = tile + decode_at(plus, plus_scale, there * 2 + j, 8)
                    tile = tile + decode_at(minus, minus_scale, there * 2 + 1 - j, 8)
                    for message, scale in zip(sides, side_scales):
                        tile = tile + decode(message, scale, len(sums))
                    sums.append(tile)
        return sums

    def side_item(k, g):
        encode(mid_sums(k, g, ()), side_out.at[(k - 1) * 2 + g])
        side(k, g).start()

    def mid_item(k, h, g, extra):
        sums = mid_sums(k, g, extra)
        kk = 2 - g
        for o in range(2):
            encode(sums[o * 4 : o * 4 + 2], mid_out.at[(h * 2 + o) * 3 + kk - 1])
            encode(sums[o * 4 + 2 : o * 4 + 4], mid_out.at[((h * 2 + o) * 3 + 2) * (1 - g) + 12 * g])
            for j in range(2):
                own_sum[h * 4 + o * 2 + j] = sums[o * 4 + 2 + j]
        for o in range(2):
            mid(h, turned(o, r), kk).start()

        @pl.when(g == 0)
        def _():
            for o in range(2):
                mid(h, turned(o, r), 3).start()

    def own_item(h):
        sums = []
        for o in range(2):
            messages = []
            for kk in range(1, 4):
                mid(h, o, kk).wait_recv()
                message = mid_in.at[(h * 2 + o) * 3 + kk - 1]
                messages.append((message, scales(message, 2)))
            for j in range(2):
                tile = own_sum[h * 4 + o * 2 + j]
                for message, scale in messages:
                    tile = tile + decode(message, scale, j)
                sums.append(tile)
        if h == 0:
            encode(sums, last_out)
            last.start()
        else:
            for i, tile in enumerate(sums):
                own_sum[4 + i] = tile

    def take_p():
        to_partner.wait_recv()
        forward.start()
        for copy in pairs_over:
            copy.wait_recv()
        for copy in pair_moves:
            copy.start()

    def spread_p():
        for copy in pair_moves:
            copy.wait()
        forward_in.wait_recv()

        @pl.loop(0, 32)
        def _(i):
            p_all[32 + i] = p_land[i]

    @pl.loop(0, len(ITEMS))
    def _(i):
        word = 0
        for n in range(0, len(ITEMS), 4):
            codes = [((item[0] * 4 + item[1]) * 2 + item[2]) * 2 + item[3] for item in ITEMS[n : n + 4]]
            word = jnp.where(i // 4 == n // 4, sum(code << (7 * at) for at, code in enumerate(codes)), word)
        code = (word >> (7 * (i % 4))) & 127
        kind, k, u, d = code // 16, (code // 4) % 4, (code // 2) % 2, code % 2
        pl.when(kind == FAR)(lambda: far_item(k, turned(u, r)))
        pl.when(kind == NEAR)(lambda: near_item(k, turned(u, r), turned(d, r)))

        @pl.when(kind >= SIDE)
        def _():
            pl.when(kind == SIDE)(lambda: side_item(k, u))
            pl.when(kind == MID)(lambda: mid_item(3, 0, u, ()))
            pl.when(kind == HOME)(lambda: mid_item(0, 1, u, (1, 2)))
            pl.when(kind == TAKE)(take_p)
            pl.when(kind == SPREAD)(spread_p)
            pl.when(kind == OWN)(lambda: own_item(0))
    own_item(1)

    last.wait_recv()
    scale = scales(last_in, 4)
    for i in range(4):
        out[i] = (own_sum[4 + i] + decode(last_in, scale, i)).astype(out.dtype)

    for copy in (to_sibling, to_partner, forward, *pairs_over, last):
        copy.wait_send()

    @pl.loop(0, 16)
    def _(i):
        far(i // 4, (i // 2) % 2, i % 2).wait_send()
        near(i // 4, (i // 2) % 2, i % 2).wait_send()

    for k in (1, 2):
        for g in range(2):
            side(k, g).wait_send()
    for h in range(2):
        for o in range(2):
            for kk in range(1, 4):
                mid(h, o, kk).wait_send()


def on_device(a_tiles, p_tiles, pair_a, pair_p):
    lists = [jnp.transpose(pair[0, 0, 0], (0, 2, 1)) for pair in (pair_a, pair_p)]
    i16 = jnp.int16
    dma = pltpu.SemaphoreType.DMA
    vmem = pl.BlockSpec(memory_space=pltpu.VMEM)
    anywhere = pl.BlockSpec(memory_space=pl.ANY)
    out = pl.pallas_call(
        kernel,
        out_shape=jax.ShapeDtypeStruct((4, TB, TB), jnp.bfloat16),
        in_specs=[anywhere] * 4,
        out_specs=vmem,
        scratch_shapes=[
            pltpu.VMEM((64, TB, TB), jnp.bfloat16),
            pltpu.VMEM((64, TB, TB), jnp.bfloat16),
            pltpu.VMEM((32, TB, TB), jnp.bfloat16),
            pltpu.VMEM((2, 16, TB), jnp.int32),
            pltpu.SMEM((32, TB), jnp.int32),
            pltpu.SMEM((32, TB), jnp.int32),
            pltpu.VMEM((8, TB, TB), jnp.float32),
            pltpu.VMEM((16, HALF, TB), i16),
            pltpu.VMEM((16, HALF, TB), i16),
            pltpu.VMEM((16, FULL, TB), i16),
            pltpu.VMEM((16, FULL, TB), i16),
            pltpu.VMEM((4, FULL, TB), i16),
            pltpu.VMEM((4, FULL, TB), i16),
            pltpu.VMEM((13, PAIR, TB), i16),
            pltpu.VMEM((12, PAIR, TB), i16),
            pltpu.VMEM((HALF, TB), i16),
            pltpu.VMEM((HALF, TB), i16),
            dma((6,)), dma((3,)), dma((3,)), dma((2,)), dma((2,)),
            dma((16,)), dma((16,)), dma((16,)), dma((16,)),
            dma((4,)), dma((4,)), dma((12,)), dma((12,)), dma, dma,
        ],
        compiler_params=pltpu.CompilerParams(
            collective_id=0, has_side_effects=True, vmem_limit_bytes=56 << 20
        ),
        cost_estimate=pl.CostEstimate(flops=2 * 4096 * TB**3, bytes_accessed=4 << 20, transcendentals=0),
    )(*lists, a_tiles[0, 0, 0], p_tiles[0, 0, 0])
    return out[None, None]


def solution(mesh):
    tiles = P("row", "col", "layer", None, None, None)
    return jax.shard_map(
        on_device, mesh=mesh, in_specs=(tiles,) * 4,
        out_specs=P("row", "col", "layer", None, None), check_vma=False,
    )
```
